32 devices in a mesh: section: 2 (over core), dp: 4 (over z), seq: 4 (over y, x).
Axes of the slice: x: 2, y: 2, z: 4, core: 2. Of those that a mesh axis runs over, the one named last changes fastest.
Arguments:
- section_input: bfloat16 [8, 640, 768], P('dp', 'seq'), may hold values from -6 to 6
- out_cotangent: bfloat16 [8, 640, 768], P('dp', 'seq'), may hold values from -6 to 6
- lengths: int32 [8], P('dp'), may hold values from 481 to 577
- attn_gain: bfloat16 [2, 768], P('section'), may hold values from 0.25 to 1.75
- w_query: bfloat16 [2, 768, 768], P('section'), may hold values from -0.21875 to 0.21875
- w_key: bfloat16 [2, 768, 768], P('section'), may hold values from -0.21875 to 0.21875
- w_value: bfloat16 [2, 768, 768], P('section'), may hold values from -0.21875 to 0.21875
- w_output: bfloat16 [2, 768, 768], P('section'), may hold values from -3.5 to 3.5
- ffn_gain: bfloat16 [2, 768], P('section'), may hold values from 0.25 to 1.75
- w_gate: bfloat16 [2, 768, 2048], P('section'), may hold values from -0.21875 to 0.21875
- w_up: bfloat16 [2, 768, 2048], P('section'), may hold values from -0.21875 to 0.21875
- w_down: bfloat16 [2, 2048, 768], P('section'), may hold values from -0.125 to 0.125
Outputs:
- section_outputs: bfloat16 [2, 8, 640, 768], P('section', 'dp', 'seq')
- input_grads: bfloat16 [2, 8, 640, 768], P('section', 'dp', 'seq')
- grad_attn_gain: float32 [2, 768], P('section', ('dp', 'seq'))
- grad_query: float32 [2, 768, 768], P('section', 'dp', 'seq')
- grad_key: float32 [2, 768, 768], P('section', 'dp', 'seq')
- grad_value: float32 [2, 768, 768], P('section', 'dp', 'seq')
- grad_output: float32 [2, 768, 768], P('section', 'dp', 'seq')
- grad_ffn_gain: float32 [2, 768], P('section', ('dp', 'seq'))
- grad_gate: float32 [2, 768, 2048], P('section', 'dp', 'seq')
- grad_up: float32 [2, 768, 2048], P('section', 'dp', 'seq')
- grad_down: float32 [2, 2048, 768], P('section', 'dp', 'seq')
The draws below stay inside these ranges and needn't reach their ends.
All inputs are finite; a program needn't handle non-finite values.
Results may differ from the reference program's by a relative error of at most 0.025.
Values may be sent and summed in bfloat16 or wider, within the bound.
No kernel may reach another device: no remote copies, remote signals or barrier semaphores. Data moves between devices by JAX's collectives and lax.ppermute only.
A program may use at most 192 MiB of HBM per device.

```python
import jax
import jax.numpy as jnp
from jax import lax

D = 768
HEADS = 12
HEAD_DIM = 64
FF = 2048
SLOTS = 640
PAD = 63
ITEMS = 8
SLOT_DEV = 160


def touch_ends(result, key, low, high):
    longest = result.shape.index(max(result.shape))
    spots = []
    for shift in (0, 1):
        where = [jax.random.randint(jax.random.fold_in(key, axis), (), 0, length) for axis, length in enumerate(result.shape)]
        where[longest] = (where[longest] + shift) % result.shape[longest]
        spots.append(tuple(where))
    return result.at[spots[0]].set(low).at[spots[1]].set(high)


def shard_levels(rng, dims, split, smallest, top_value):
    factor_of, own = 1.0, jax.random.fold_in(rng, 6)
    for axis_at, shards_of in split:
        heights = jnp.exp(jax.random.uniform(jax.random.fold_in(own, axis_at), (shards_of,), jnp.float32, smallest / len(split), top_value / len(split)))
        factor_of = factor_of * jnp.repeat(heights, dims[axis_at] // shards_of).reshape([-1 if axis == axis_at else 1 for axis in range(len(dims))])
    return factor_of


def normal_values(key, extent, width, bound, split=(), kind=jnp.bfloat16):
    result = width * jax.random.normal(key, extent, jnp.float32)
    if split:
        result = result * shard_levels(key, extent, split, -0.22, 0.18)
    return jnp.clip(result, -bound, bound).astype(kind)


def setup_inputs(seed: int = 0) -> dict:
    keys = jax.random.split(jax.random.key(seed), 13)
    return {
        "section_input": normal_values(keys[0], (ITEMS, SLOTS, D), 1.0, 6.0, ((0, 4), (1, 4))),
        "out_cotangent": normal_values(keys[1], (ITEMS, SLOTS, D), 1.0, 6.0, ((0, 4), (1, 4))),
        "lengths": touch_ends(jax.random.randint(keys[2], (ITEMS,), SLOTS - SLOT_DEV + 1, SLOTS - PAD + 1), jax.random.fold_in(keys[2], 1), SLOTS - SLOT_DEV + 1, SLOTS - PAD).astype(jnp.int32),
        "attn_gain": jnp.clip(1.0 + 0.15 * jax.random.normal(keys[3], (2, D), jnp.float32), 0.25, 1.75).astype(jnp.bfloat16),
        "w_query": normal_values(keys[4], (2, D, D), D ** -0.5, 0.21875, ((0, 2),)),
        "w_key": normal_values(keys[5], (2, D, D), D ** -0.5, 0.21875, ((0, 2),)),
        "w_value": normal_values(keys[6], (2, D, D), D ** -0.5, 0.21875, ((0, 2),)),
        "w_output": normal_values(keys[7], (2, D, D), (max(D // 256, 1)) ** -0.5, 3.5, ((0, 2),)),
        "ffn_gain": jnp.clip(1.0 + 0.15 * jax.random.normal(keys[8], (2, D), jnp.float32), 0.25, 1.75).astype(jnp.bfloat16),
        "w_gate": normal_values(keys[9], (2, D, FF), D ** -0.5, 0.21875, ((0, 2),)),
        "w_up": normal_values(keys[10], (2, D, FF), D ** -0.5, 0.21875, ((0, 2),)),
        "w_down": normal_values(keys[11], (2, FF, D), FF ** -0.5, 0.125, ((0, 2),)),
    }


epsilon = 1e-05
masked_score = -1e+30
highest = lax.Precision.HIGHEST

@jax.custom_vjp
def low(v):
    return lax.optimization_barrier(v.astype(jnp.bfloat16)).astype(jnp.float32)

@jax.custom_vjp
def low_back(v):
    return v

def low_keep(v):
    return (low(v), None)

def low_pass(kept, grad):
    return (grad,)

def back_keep(v):
    return (v, None)

def back_low(kept, grad):
    return (low(grad),)
low.defvjp(low_keep, low_pass)
low_back.defvjp(back_keep, back_low)

def rotary_tables(count_rows, first_slot, head_dim):
    half_dim = head_dim // 2
    frequency = 10000.0 ** (-2.0 * jnp.arange(half_dim, dtype=jnp.float32) / head_dim)
    places = (first_slot + jnp.arange(count_rows, dtype=jnp.int32)).astype(jnp.float32)
    angles = places[:, None] * frequency[None, :]
    return (jnp.cos(angles), jnp.sin(angles))

def rotate(inputs, cosine, sine_table, direction):
    half_dim = inputs.shape[-1] // 2
    first_half = inputs[..., :half_dim]
    second_half = inputs[..., half_dim:]
    cos_wide = cosine[None, :, None, :]
    sin_wide = direction * sine_table[None, :, None, :]
    return jnp.concatenate([first_half * cos_wide - second_half * sin_wide, first_half * sin_wide + second_half * cos_wide], axis=-1)

def rms_norm(inputs, gain_row):
    return inputs * lax.rsqrt(lax.optimization_barrier(jnp.mean(inputs * inputs, axis=-1, keepdims=True)) + epsilon) * gain_row

def linear(inputs, matrix):
    return jnp.einsum('bsd,de->bse', inputs, matrix, precision=highest)

def attend_item(packed):
    queries, key_heads, value_heads, length = packed
    scores = jnp.einsum('qhd,khd->hqk', queries, key_heads, precision=highest) * HEAD_DIM ** (-0.5)
    places = jnp.arange(SLOTS, dtype=jnp.int32)
    allowed = (places[None, :] <= places[:, None]) & (places[None, :] < length)
    scores = low_back(jnp.where(allowed[None], scores, masked_score))
    attention = low(jax.nn.softmax(scores, axis=-1))
    return jnp.einsum('hqk,khd->qhd', attention, value_heads, precision=highest)

def layer(inputs, params, item_lengths):
    attn_gain, w_query, w_key, w_value, w_output, ffn_gain, w_gate, w_up, w_down = params
    batch_size = inputs.shape[0]
    heads_shape = (batch_size, SLOTS, HEADS, HEAD_DIM)
    cosine, sine_table = rotary_tables(SLOTS, 0, HEAD_DIM)
    normed = low(rms_norm(inputs, attn_gain))
    queries = low_back(linear(normed, w_query)).reshape(heads_shape)
    key_proj = low_back(linear(normed, w_key)).reshape(heads_shape)
    value_proj = low_back(low(linear(normed, w_value))).reshape(heads_shape)
    query_rot = low(rotate(queries, cosine, sine_table, 1.0))
    key_rot = low(rotate(key_proj, cosine, sine_table, 1.0))
    mixed = lax.map(jax.checkpoint(attend_item), (query_rot, key_rot, value_proj, item_lengths))
    mixed = low_back(low(mixed.reshape(batch_size, SLOTS, D)))
    after_attn = inputs + low_back(linear(mixed, w_output))
    normed_two = low(rms_norm(after_attn, ffn_gain))
    gate_proj = low_back(linear(normed_two, w_gate))
    up_proj = low_back(linear(normed_two, w_up))
    hidden = low(jax.nn.silu(gate_proj) * up_proj)
    return after_attn + low_back(linear(hidden, w_down))

def reference(section_input, out_cotangent, lengths, attn_gain, w_query, w_key, w_value, w_output, ffn_gain, w_gate, w_up, w_down):
    stacked = tuple((weight.astype(jnp.float32) for weight in (attn_gain, w_query, w_key, w_value, w_output, ffn_gain, w_gate, w_up, w_down)))
    layer_zero = tuple((weight[0] for weight in stacked))
    layer_one = tuple((weight[1] for weight in stacked))
    groups = ITEMS // 4
    inputs = section_input.astype(jnp.float32).reshape(groups, 4, SLOTS, D)
    cotangents = out_cotangent.astype(jnp.float32).reshape(groups, 4, SLOTS, D)
    group_lengths = lengths.reshape(groups, 4)

    def one_group(totals, packed):
        group_in, group_cot, group_len = packed
        middle, back_zero = jax.vjp(lambda block_in, weights: layer(block_in, weights, group_len), group_in, layer_zero)
        middle_low = low(middle)
        final, back_one = jax.vjp(lambda block_in, weights: layer(block_in, weights, group_len), middle_low, layer_one)
        grad_middle, grads_one = back_one(group_cot)
        grad_middle_low = low(grad_middle)
        grad_input, grads_zero = back_zero(grad_middle_low)
        totals = tuple((running + jnp.stack([first_grad, second_grad]) for running, first_grad, second_grad in zip(totals, grads_zero, grads_one)))
        return (totals, (middle_low, final, grad_input, grad_middle_low))
    start_totals = tuple((jnp.zeros_like(weight) for weight in stacked))
    totals, (middles, finals, grad_inputs, grad_middles) = lax.scan(one_group, start_totals, (inputs, cotangents, group_lengths))
    section_outputs = jnp.stack([middles, finals]).reshape(2, ITEMS, SLOTS, D).astype(jnp.bfloat16)
    input_grads = jnp.stack([grad_inputs, grad_middles]).reshape(2, ITEMS, SLOTS, D).astype(jnp.bfloat16)
    return (section_outputs, input_grads, totals[0], totals[1], totals[2], totals[3], totals[4], totals[5], totals[6], totals[7], totals[8])
```

```python
import functools

import jax
import jax.numpy as jnp
import numpy as np
from jax import lax
from jax.experimental import pallas as pl
from jax.experimental.pallas import tpu as pltpu
from jax.sharding import PartitionSpec as P

DIM = 768
HEAD_DIM = 64
FF = 2048
ROWS = 160
PARTS = 4
SLOTS = ROWS * PARTS
SHARE_HEADS = 3
SHARE = SHARE_HEADS * HEAD_DIM
FF_SHARE = FF // PARTS
PACKED = SLOTS * 3 // 2
PACKED_ROWS = ROWS * 3 // 2
WINDOW = 256
QUERY_BLOCKS = ((0, 256), (256, 256), (512, 128))
HALVES = ((0, 320), (320, 320))

epsilon = 1e-05
masked_score = -1e30
bf16 = jnp.bfloat16
f32 = jnp.float32
MIB = 1 << 20


def nn(left, right):
    return lax.dot_general(left, right, (((1,), (0,)), ((), ())), preferred_element_type=f32)


def nt(left, right):
    return lax.dot_general(left, right, (((1,), (1,)), ((), ())), preferred_element_type=f32)


def tn(left, right):
    return lax.dot_general(left, right, (((0,), (0,)), ((), ())), preferred_element_type=f32)


def rms_scale(values):
    return lax.rsqrt(jnp.mean(values * values, axis=-1, keepdims=True) + epsilon)


def rotate(values, cosine, signed_sine):
    width = values.shape[-1]
    lane = lax.broadcasted_iota(jnp.int32, values.shape, 1)
    ahead = pltpu.roll(values, width - 32, 1)
    behind = pltpu.roll(values, 32, 1)
    partner = jnp.where(lane % HEAD_DIM < 32, ahead, behind)
    return values * cosine + partner * signed_sine


def wide(table):
    return jnp.concatenate([table, table], axis=1)


def unpack(packed, count):
    tail = packed[count:]
    third = jnp.concatenate([tail[:, :HEAD_DIM], tail[:, HEAD_DIM:]], axis=0)
    return jnp.concatenate([packed[:count], third], axis=1)


def place():
    return lax.axis_index("section"), lax.axis_index("seq")


def block_rows(index, size=ROWS):
    return pl.ds(pl.multiple_of(index * size, size), size)


def window_start(seq):
    return pl.multiple_of(((3 * seq) >> 1) * 128, 128)


class Loader:
    def __init__(self, sems, core):
        self.sems = sems
        self.core = core
        self.count = 0

    def start(self, layer, own, other, target):
        sem = self.sems.at[self.count]
        self.count += 1

        @pl.when(self.core == layer)
        def _():
            pltpu.make_async_copy(own, target, sem).start()

        @pl.when(self.core != layer)
        def _():
            pltpu.make_async_copy(other, target, sem).start()

        return pltpu.make_async_copy(own, target, sem)


def project(normed, windows, odd, cos, sin, queries, keys, values, value_t):
    for first, count in QUERY_BLOCKS:
        rows = slice(first, first + count)
        block = normed[rows, :]
        cosine, sine = wide(cos[rows, :]), wide(sin[rows, :])
        for kind, (window, target) in enumerate(zip(windows, (queries, keys, values))):
            result = nn(block, window[...])
            if kind < 2:
                result = rotate(result, cosine, sine)
            if kind == 0:
                result = result * HEAD_DIM ** (-0.5)
            result = jnp.where(odd, pltpu.roll(result, WINDOW - HEAD_DIM, 1), result)
            low = result.astype(bf16)
            for head in range(SHARE_HEADS):
                target[head, rows, :] = low[:, head * HEAD_DIM : (head + 1) * HEAD_DIM]
            if kind == 2:
                turned = jnp.transpose(result).astype(bf16)
                for head in range(SHARE_HEADS):
                    value_t[head, :, rows] = turned[head * HEAD_DIM : (head + 1) * HEAD_DIM, :]


def masked(scores_t, first, length):
    spots = lax.broadcasted_iota(jnp.int32, scores_t.shape, 0)
    query = first + lax.broadcasted_iota(jnp.int32, (1, scores_t.shape[1]), 1)
    bound = jnp.minimum(query + 1, length)
    return jnp.where(spots < bound, scores_t, masked_score)


def attend(queries, keys, value_t, length, mixed_t):
    @pl.loop(0, SHARE_HEADS)
    def _(head):
        for first, count in QUERY_BLOCKS:
            last = first + count
            scores = nt(keys[head, :last, :], queries[head, first:last, :])
            scores = masked(scores, first, length)
            exponent = jnp.exp(scores - jnp.max(scores, axis=0, keepdims=True))
            total = jnp.sum(exponent, axis=0, keepdims=True)
            mixed = nn(value_t[head, :, :last], exponent.astype(bf16))
            mixed_t[head, :, first:last] = mixed * (1.0 / total)


def untranspose(mixed_t, pair, single):
    both = jnp.concatenate([mixed_t[0], mixed_t[1]], axis=0)
    pair[...] = jnp.transpose(both).astype(bf16)
    last = jnp.concatenate([mixed_t[2], mixed_t[2]], axis=0)
    single[...] = jnp.transpose(last).astype(bf16)


def pack_all(pair, single, target):
    half = SLOTS // 2
    target[:SLOTS, :] = pair[...]
    target[SLOTS:, :] = jnp.concatenate(
        [single[:half, :HEAD_DIM], single[half:, :HEAD_DIM]], axis=1
    )


def pack_block(pair, single, index, target):
    half = ROWS // 2
    rows = block_rows(index)
    target[:ROWS, :] = pair[rows, :]
    tail = single[rows, :]
    target[ROWS:, :] = jnp.concatenate([tail[:half, :HEAD_DIM], tail[half:, :HEAD_DIM]], axis=1)


def norm_back(grad_normed, gain, normed, scale):
    scaled = grad_normed * gain
    return scale * (scaled - normed * jnp.mean(scaled * normed, axis=-1, keepdims=True))


def ffn_back_chunk(gate, up, grad_hidden):
    sigmoid = jax.nn.sigmoid(gate)
    grad_gate = grad_hidden * up * sigmoid * (1.0 + gate * (1.0 - sigmoid))
    grad_up = grad_hidden * gate * sigmoid
    return grad_gate.astype(bf16), grad_up.astype(bf16)


def first_attention(
    x_0, x_1, x_2, x_3, length, gain_own, gain_other, cos, sin,
    q_own, q_other, k_own, k_other, v_own, v_other,
    normed, queries, keys, values, packed,
    w_q, w_k, w_v, value_t, mixed_t, pair, single, sems,
):
    core, seq = place()
    odd = seq % 2 == 1
    loader = Loader(sems, core)
    span = pl.ds(window_start(seq), WINDOW)
    copies = [
        loader.start(0, own.at[0, :, span], other.at[0, :, span], target)
        for own, other, target in ((q_own, q_other, w_q), (k_own, k_other, w_k), (v_own, v_other, w_v))
    ]
    gain = jnp.where(core == 0, gain_own[0:1, :], gain_other[0:1, :])
    for offset, block in enumerate((x_0, x_1, x_2, x_3)):
        wide_block = block[...].astype(f32)
        normed[block_rows(seq ^ offset), :] = (wide_block * rms_scale(wide_block) * gain).astype(bf16)
    for copy in copies:
        copy.wait()
    project(normed, (w_q, w_k, w_v), odd, cos, sin, queries, keys, values, value_t)
    attend(queries, keys, value_t, length[0], mixed_t)
    untranspose(mixed_t, pair, single)
    pack_all(pair, single, packed)


def middle(
    x_0, x_1, x_2, x_3, o_0, o_1, o_2, o_3, length, gain_own, gain_other, cos, sin,
    o_own, o_other, g_own, g_other, u_own, u_other, d_own, d_other,
    q_own, q_other, k_own, k_other, v_own, v_other,
    after_own, normed_two, hidden, mid_own, normed, queries, keys, values, packed,
    b_0, b_1, b_2, b_3,
    w_o, w_g, w_u, w_d, w_q, w_k, w_v, after, total, value_t, mixed_t, pair, single, sems,
):
    core, seq = place()
    odd = seq % 2 == 1
    loader = Loader(sems, core)
    copy_o = loader.start(0, o_own.at[0], o_other.at[0], w_o)
    copies = []
    for part in range(PARTS):
        span = slice(part * FF_SHARE, (part + 1) * FF_SHARE)
        copies.append(
            (
                loader.start(0, g_own.at[0, :, span], g_other.at[0, :, span], w_g.at[part]),
                loader.start(0, u_own.at[0, :, span], u_other.at[0, :, span], w_u.at[part]),
                loader.start(0, d_own.at[0, span, :], d_other.at[0, span, :], w_d.at[span, :]),
            )
        )
    span = pl.ds(window_start(seq), WINDOW)
    copies_qkv = [
        loader.start(1, own.at[0, :, span], other.at[0, :, span], target)
        for own, other, target in ((q_own, q_other, w_q), (k_own, k_other, w_k), (v_own, v_other, w_v))
    ]
    gain_ffn = jnp.where(core == 0, gain_own[1:2, :], gain_other[1:2, :])
    gain_attn = jnp.where(core == 1, gain_own[0:1, :], gain_other[0:1, :])
    for offset, block in enumerate((x_0, x_1, x_2, x_3)):
        after[block_rows(seq ^ offset), :] = block[...].astype(f32)
    copy_o.wait()
    for offset, block in enumerate((o_0, o_1, o_2, o_3)):
        share = w_o[block_rows(seq ^ offset, SHARE), :]
        whole = unpack(block[...], SLOTS)
        for first, count in HALVES:
            rows = slice(first, first + count)
            after[rows, :] += nn(whole[rows], share)
    for first, count in HALVES:
        rows = slice(first, first + count)
        block = after[rows, :]
        normed_two[rows, :] = (block * rms_scale(block) * gain_ffn).astype(bf16)
        total[rows, :] = block
    after_own[...] = after[block_rows(seq), :]
    for part in range(PARTS):
        for copy in copies[part]:
            copy.wait()
        for first, count in HALVES:
            rows = slice(first, first + count)
            block = normed_two[rows, :]
            gate = nn(block, w_g[part])
            up = nn(block, w_u[part])
            low = (gate * jax.nn.sigmoid(gate) * up).astype(bf16)
            hidden[rows, part * FF_SHARE : (part + 1) * FF_SHARE] = low
            total[rows, :] += nn(low, w_d[part * FF_SHARE : (part + 1) * FF_SHARE, :])
    for first, count in HALVES:
        rows = slice(first, first + count)
        low = total[rows, :].astype(bf16)
        block = low.astype(f32)
        total[rows, :] = block
        normed[rows, :] = (block * rms_scale(block) * gain_attn).astype(bf16)
    mid_own[...] = total[block_rows(seq), :].astype(bf16)
    for copy in copies_qkv:
        copy.wait()
    project(normed, (w_q, w_k, w_v), odd, cos, sin, queries, keys, values, value_t)
    attend(queries, keys, value_t, length[0], mixed_t)
    untranspose(mixed_t, pair, single)
    pack_all(pair, single, packed)
    for offset, target in enumerate((b_0, b_1, b_2, b_3)):
        pack_block(pair, single, seq ^ offset, target)


def send_blocks(seq, grad_branch, w_o, targets):
    for here in range(PARTS):

        @pl.when(seq == here)
        def _():
            for offset, target in enumerate(targets):
                other = here ^ offset
                span = slice(other * SHARE, (other + 1) * SHARE)
                grad_heads = nt(grad_branch, w_o[span, :]).astype(bf16)
                target[...] = jnp.concatenate([grad_heads, grad_branch[:, span]], axis=1)


def last_rows(
    mid_own, cotangent, o_0, o_1, o_2, o_3, gain_own, gain_other,
    o_own, o_other, g_own, g_other, u_own, u_other, d_own, d_other,
    output, normed_two, grad_after, grad_gain, b_0, b_1, b_2, b_3,
    w_o, w_g, w_u, w_d, branch, hidden, sems,
):
    core, seq = place()
    loader = Loader(sems, core)
    copy_o = loader.start(1, o_own.at[0], o_other.at[0], w_o)
    copies = []
    for part in range(PARTS):
        span = slice(part * FF_SHARE, (part + 1) * FF_SHARE)
        copies.append(
            (
                loader.start(1, g_own.at[0, :, span], g_other.at[0, :, span], w_g.at[part]),
                loader.start(1, u_own.at[0, :, span], u_other.at[0, :, span], w_u.at[part]),
                loader.start(1, d_own.at[0, span, :], d_other.at[0, span, :], w_d.at[span, :]),
            )
        )
    gain = jnp.where(core == 1, gain_own[1:2, :], gain_other[1:2, :])
    copy_o.wait()
    after = mid_own[...].astype(f32)
    for offset, block in enumerate((o_0, o_1, o_2, o_3)):
        after = after + nn(unpack(block[...], ROWS), w_o[block_rows(seq ^ offset, SHARE), :])
    scale = rms_scale(after)
    normed = after * scale
    low = (normed * gain).astype(bf16)
    normed_two[...] = low
    grad_low = cotangent[...]
    grad_normed = jnp.zeros((ROWS, DIM), f32)
    for part in range(PARTS):
        for copy in copies[part]:
            copy.wait()
        gate = nn(low, w_g[part])
        up = nn(low, w_u[part])
        span = slice(part * FF_SHARE, (part + 1) * FF_SHARE)
        hidden[:, span] = (gate * jax.nn.sigmoid(gate) * up).astype(bf16)
        grad_gate, grad_up = ffn_back_chunk(gate, up, nt(grad_low, w_d[span, :]))
        grad_normed = grad_normed + nt(grad_gate, w_g[part]) + nt(grad_up, w_u[part])
    output[...] = (after + nn(hidden[...], w_d[...])).astype(bf16)
    grad_gain[...] = jnp.sum(grad_normed * normed, axis=0, keepdims=True)
    total = grad_low.astype(f32) + norm_back(grad_normed, gain, normed, scale)
    grad_after[...] = total
    branch[...] = total.astype(bf16)
    send_blocks(seq, branch[...], w_o, (b_0, b_1, b_2, b_3))


def first_rows_back(
    after_own, grad_in, gain_own, gain_other,
    o_own, o_other, g_own, g_other, u_own, u_other, d_own, d_other,
    grad_after, grad_gain, b_0, b_1, b_2, b_3,
    w_o, w_g, w_u, w_d, branch, sems,
):
    core, seq = place()
    loader = Loader(sems, core)
    copies = []
    for part in range(PARTS):
        span = slice(part * FF_SHARE, (part + 1) * FF_SHARE)
        copies.append(
            (
                loader.start(0, g_own.at[0, :, span], g_other.at[0, :, span], w_g.at[part]),
                loader.start(0, u_own.at[0, :, span], u_other.at[0, :, span], w_u.at[part]),
                loader.start(0, d_own.at[0, span, :], d_other.at[0, span, :], w_d.at[span, :]),
            )
        )
    copy_o = loader.start(0, o_own.at[0], o_other.at[0], w_o)
    gain = jnp.where(core == 0, gain_own[1:2, :], gain_other[1:2, :])
    after = after_own[...]
    scale = rms_scale(after)
    normed = after * scale
    low = (normed * gain).astype(bf16)
    grad_low = grad_in[...]
    grad_normed = jnp.zeros((ROWS, DIM), f32)
    for part in range(PARTS):
        for copy in copies[part]:
            copy.wait()
        gate = nn(low, w_g[part])
        up = nn(low, w_u[part])
        grad_gate, grad_up = ffn_back_chunk(gate, up, nt(grad_low, w_d[part * FF_SHARE : (part + 1) * FF_SHARE, :]))
        grad_normed = grad_normed + nt(grad_gate, w_g[part]) + nt(grad_up, w_u[part])
    grad_gain[...] = jnp.sum(grad_normed * normed, axis=0, keepdims=True)
    total = grad_low.astype(f32) + norm_back(grad_normed, gain, normed, scale)
    grad_after[...] = total
    branch[...] = total.astype(bf16)
    copy_o.wait()
    send_blocks(seq, branch[...], w_o, (b_0, b_1, b_2, b_3))


def attention_back(
    g_0, g_1, g_2, g_3, length, cos, sin, queries, keys, values,
    b_0, b_1, b_2, b_3,
    grad_mixed, key_t, query_grad_t, key_grad, value_grad, whole,
):
    _, seq = place()
    for offset, block in enumerate((g_0, g_1, g_2, g_3)):
        low = block[:, :SHARE]
        for head in range(SHARE_HEADS):
            grad_mixed[head, block_rows(seq ^ offset), :] = low[:, head * HEAD_DIM : (head + 1) * HEAD_DIM]
    key_grad[...] = jnp.zeros_like(key_grad)
    value_grad[...] = jnp.zeros_like(value_grad)

    @pl.loop(0, SHARE_HEADS)
    def _(head):
        key_wide = keys[head].astype(f32)
        key_t[...] = jnp.transpose(jnp.concatenate([key_wide, key_wide], axis=1))[:HEAD_DIM].astype(bf16)
        for first, count in QUERY_BLOCKS:
            last = first + count
            query = queries[head, first:last, :]
            grad = grad_mixed[head, first:last, :]
            scores = nt(keys[head, :last, :], query)
            scores = masked(scores, first, length[0])
            exponent = jnp.exp(scores - jnp.max(scores, axis=0, keepdims=True))
            weights = exponent * (1.0 / jnp.sum(exponent, axis=0, keepdims=True))
            grad_weights = nt(values[head, :last, :], grad)
            row_total = jnp.sum(weights * grad_weights, axis=0, keepdims=True)
            grad_scores = (weights * (grad_weights - row_total)).astype(bf16)
            value_grad[head, :last, :] += nn(weights.astype(bf16), grad)
            key_grad[head, :last, :] += nn(grad_scores, query)
            query_grad_t[head, :, first:last] = nn(key_t[:, :last], grad_scores) * HEAD_DIM ** (-0.5)

    turned = jnp.concatenate([query_grad_t[0], query_grad_t[1], query_grad_t[2], query_grad_t[2]], axis=0)
    query_side = jnp.transpose(turned)
    key_side = jnp.concatenate([key_grad[0], key_grad[1], key_grad[2], key_grad[2]], axis=1)
    value_side = jnp.concatenate([value_grad[0], value_grad[1], value_grad[2]], axis=1)
    cosine, sine = wide(cos[...]), wide(sin[...])
    query_side = rotate(query_side, cosine, -sine)[:, :SHARE]
    key_side = rotate(key_side, cosine, -sine)[:, :SHARE]
    whole[...] = jnp.concatenate([query_side, key_side, value_side], axis=1).astype(bf16)
    for offset, target in enumerate((b_0, b_1, b_2, b_3)):
        target[...] = whole[block_rows(seq ^ offset), :]


def input_back(
    layer, b_0, b_1, b_2, b_3, inputs, grad_after, gain_own, gain_other,
    q_own, q_other, k_own, k_other, v_own, v_other,
    grad_in, grad_gain,
    w_q, w_k, w_v, sides, sems,
):
    core, seq = place()
    loader = Loader(sems, core)
    copies = [
        loader.start(layer, own.at[0], other.at[0], target)
        for own, other, target in ((q_own, q_other, w_q), (k_own, k_other, w_k), (v_own, v_other, w_v))
    ]
    gain = jnp.where(core == layer, gain_own[0:1, :], gain_other[0:1, :])
    blocks = (b_0, b_1, b_2, b_3)
    for here in range(PARTS):

        @pl.when(seq == here)
        def _():
            for kind in range(3):
                span = slice(kind * SHARE, (kind + 1) * SHARE)
                sides[kind] = jnp.concatenate(
                    [blocks[here ^ part][:, span] for part in range(PARTS)], axis=1
                )

    wide_inputs = inputs[...].astype(f32)
    scale = rms_scale(wide_inputs)
    normed = wide_inputs * scale
    grad_normed = jnp.zeros((ROWS, DIM), f32)
    for kind, weight in enumerate((w_q, w_k, w_v)):
        copies[kind].wait()
        grad_normed = grad_normed + nt(sides[kind], weight[...])
    grad_gain[...] = jnp.sum(grad_normed * normed, axis=0, keepdims=True)
    grad_in[...] = (grad_after[...] + norm_back(grad_normed, gain, normed, scale)).astype(bf16)


def attention_weights_grad(
    normed, b_0, b_1, b_2, b_3, o_0, o_1, o_2, o_3, g_0, g_1, g_2, g_3,
    keep, send,
    whole, branch, output_grad,
):
    core, seq = place()
    for offset, (block, grad) in enumerate(zip((b_0, b_1, b_2, b_3), (g_0, g_1, g_2, g_3))):
        rows = block_rows(seq ^ offset)
        whole[rows, :] = block[...]
        branch[rows, :] = grad[:, SHARE:]
    for offset, block in enumerate((o_0, o_1, o_2, o_3)):
        output_grad[block_rows(seq ^ offset, SHARE), :] = tn(unpack(block[...], SLOTS), branch[...])
    result = tn(normed[...], whole[...])
    low = result[:, : 2 * SHARE].astype(bf16)
    high = jnp.concatenate([result[:, 2 * SHARE :], output_grad[...]], axis=1).astype(bf16)

    @pl.when(core == 0)
    def _():
        keep[...] = low
        send[...] = high

    @pl.when(core == 1)
    def _():
        keep[...] = high
        send[...] = low


def ffn_weights_grad(
    layer, groups, *refs
):
    if layer == 0:
        (normed_two, hidden, y_0, y_1, y_2, y_3, g_own, g_other, u_own, u_other, d_own, d_other,
         keep, send, keep_down, send_down,
         w_g, w_u, w_d, grad_out, grad_gate, grad_up, down, sems) = refs
    else:
        (n_0, n_1, n_2, n_3, y_0, y_1, y_2, y_3, g_own, g_other, u_own, u_other, d_own, d_other,
         keep, send, keep_down, send_down,
         w_g, w_u, w_d, normed_two, grad_out, grad_gate, grad_up, down, sems) = refs
    core, seq = place()
    loader = Loader(sems, core)
    span = pl.ds(pl.multiple_of(seq * FF_SHARE, FF_SHARE), FF_SHARE)
    last = PARTS
    copies = [
        (
            loader.start(layer, g_own.at[0, :, span], g_other.at[0, :, span], w_g.at[last]),
            loader.start(layer, u_own.at[0, :, span], u_other.at[0, :, span], w_u.at[last]),
            loader.start(layer, d_own.at[0, span, :], d_other.at[0, span, :], w_d),
        )
    ]
    if layer == 1:
        for part in range(PARTS):
            part_span = slice(part * FF_SHARE, (part + 1) * FF_SHARE)
            copies.append(
                (
                    loader.start(layer, g_own.at[0, :, part_span], g_other.at[0, :, part_span], w_g.at[part]),
                    loader.start(layer, u_own.at[0, :, part_span], u_other.at[0, :, part_span], w_u.at[part]),
                )
            )
        for offset, block in enumerate((n_0, n_1, n_2, n_3)):
            normed_two[block_rows(seq ^ offset), :] = block[...]
    for offset, block in enumerate((y_0, y_1, y_2, y_3)):
        grad_out[block_rows(seq ^ offset), :] = block[...]
    for copy in copies[0]:
        copy.wait()
    for first, count in HALVES:
        rows = slice(first, first + count)
        block = normed_two[rows, :]
        grad_gate[rows, :], grad_up[rows, :] = ffn_back_chunk(
            nn(block, w_g[last]), nn(block, w_u[last]), nt(grad_out[rows, :], w_d[...])
        )
    gate_side = tn(normed_two[...], grad_gate[...]).astype(bf16)

    @pl.when(core == 0)
    def _():
        keep[...] = gate_side

    @pl.when(core == 1)
    def _():
        send[...] = gate_side

    up_side = tn(normed_two[...], grad_up[...]).astype(bf16)

    @pl.when(core == 0)
    def _():
        send[...] = up_side

    @pl.when(core == 1)
    def _():
        keep[...] = up_side

    window = grad_out[:, pl.ds(window_start(seq), WINDOW)].astype(f32)
    columns = jnp.where(seq % 2 == 1, pltpu.roll(window, WINDOW - HEAD_DIM, 1), window)
    columns = columns[:, :SHARE].astype(bf16)
    for part in range(PARTS):
        part_span = slice(part * FF_SHARE, (part + 1) * FF_SHARE)
        if layer == 1:
            for copy in copies[1 + part]:
                copy.wait()
            pieces = []
            for first, count in HALVES:
                rows = slice(first, first + count)
                gate = nn(normed_two[rows, :], w_g[part])
                up = nn(normed_two[rows, :], w_u[part])
                pieces.append((gate * jax.nn.sigmoid(gate) * up).astype(bf16))
            low = jnp.concatenate(pieces, axis=0)
        else:
            low = hidden[:, part_span]
        down[part_span, :] = tn(low, columns)
    quarter = FF // groups // 4
    for target, half in ((keep_down, core), (send_down, 1 - core)):
        for group in range(groups):
            begin = group * 4 * quarter + half * 2 * quarter
            begin = pl.multiple_of(begin, 2 * quarter)
            target[group * quarter : (group + 1) * quarter, :] = jnp.concatenate(
                [down[pl.ds(begin, quarter), :], down[pl.ds(begin + quarter, quarter), :]], axis=1
            ).astype(bf16)


def in_vmem(count):
    return [pl.BlockSpec(memory_space=pltpu.VMEM)] * count


def anywhere(count):
    return [pl.BlockSpec(memory_space=pl.ANY)] * count


def in_smem():
    return [pl.BlockSpec(memory_space=pltpu.SMEM)]


def shape(*dims, dtype=bf16):
    return jax.ShapeDtypeStruct(dims, dtype)


def call(body, in_specs, outs, scratch, flops, vmem, name):
    return pl.pallas_call(
        body,
        out_shape=outs,
        in_specs=in_specs,
        out_specs=in_vmem(len(outs)),
        scratch_shapes=scratch,
        compiler_params=pltpu.CompilerParams(vmem_limit_bytes=vmem * MIB),
        cost_estimate=pl.CostEstimate(flops=flops, bytes_accessed=flops // 400, transcendentals=0),
        name=name,
    )


def weights_scratch():
    return [
        pltpu.VMEM((DIM, DIM), bf16),
        pltpu.VMEM((PARTS, DIM, FF_SHARE), bf16),
        pltpu.VMEM((PARTS, DIM, FF_SHARE), bf16),
        pltpu.VMEM((FF, DIM), bf16),
    ]


def windows_scratch():
    return [pltpu.VMEM((DIM, WINDOW), bf16)] * 3


def attend_scratch():
    return [
        pltpu.VMEM((SHARE_HEADS, HEAD_DIM, SLOTS), bf16),
        pltpu.VMEM((SHARE_HEADS, HEAD_DIM, SLOTS), f32),
        pltpu.VMEM((SLOTS, 128), bf16),
        pltpu.VMEM((SLOTS, 128), bf16),
    ]


def sems(count):
    return [pltpu.SemaphoreType.DMA((count,))]


HEADS_OUT = [shape(SHARE_HEADS, SLOTS, HEAD_DIM)] * 3


def call_first_attention(*args):
    return call(
        first_attention,
        in_vmem(4) + in_smem() + in_vmem(4) + anywhere(6),
        [shape(SLOTS, DIM)] + HEADS_OUT + [shape(PACKED, 128)],
        windows_scratch() + attend_scratch() + sems(3),
        4 * 10**9,
        32,
        "first_attention",
    )(*args)


def call_middle(*args):
    return call(
        middle,
        in_vmem(8) + in_smem() + in_vmem(4) + anywhere(14),
        [shape(ROWS, DIM, dtype=f32), shape(SLOTS, DIM), shape(SLOTS, FF), shape(ROWS, DIM), shape(SLOTS, DIM)]
        + HEADS_OUT
        + [shape(PACKED, 128)]
        + [shape(PACKED_ROWS, 128)] * 4,
        weights_scratch()
        + windows_scratch()
        + [pltpu.VMEM((SLOTS, DIM), f32)] * 2
        + attend_scratch()
        + sems(16),
        12 * 10**9,
        52,
        "middle",
    )(*args)


def call_last_rows(*args):
    return call(
        last_rows,
        in_vmem(8) + anywhere(8),
        [shape(ROWS, DIM), shape(ROWS, DIM), shape(ROWS, DIM, dtype=f32), shape(1, DIM, dtype=f32)]
        + [shape(ROWS, 2 * SHARE)] * 4,
        weights_scratch() + [pltpu.VMEM((ROWS, DIM), bf16), pltpu.VMEM((ROWS, FF), bf16)] + sems(13),
        6 * 10**9,
        40,
        "last_rows",
    )(*args)


def call_first_rows_back(*args):
    return call(
        first_rows_back,
        in_vmem(4) + anywhere(8),
        [shape(ROWS, DIM, dtype=f32), shape(1, DIM, dtype=f32)] + [shape(ROWS, 2 * SHARE)] * 4,
        weights_scratch() + [pltpu.VMEM((ROWS, DIM), bf16)] + sems(13),
        5 * 10**9,
        40,
        "first_rows_back",
    )(*args)


def call_attention_back(*args):
    return call(
        attention_back,
        in_vmem(4) + in_smem() + in_vmem(5),
        [shape(ROWS, 3 * SHARE)] * 4,
        [
            pltpu.VMEM((SHARE_HEADS, SLOTS, HEAD_DIM), bf16),
            pltpu.VMEM((HEAD_DIM, SLOTS), bf16),
            pltpu.VMEM((SHARE_HEADS, HEAD_DIM, SLOTS), f32),
            pltpu.VMEM((SHARE_HEADS, SLOTS, HEAD_DIM), f32),
            pltpu.VMEM((SHARE_HEADS, SLOTS, HEAD_DIM), f32),
            pltpu.VMEM((SLOTS, 3 * SHARE), bf16),
        ],
        5 * 10**9,
        40,
        "attention_back",
    )(*args)


def call_input_back(layer, *args):
    return call(
        functools.partial(input_back, layer),
        in_vmem(8) + anywhere(6),
        [shape(ROWS, DIM), shape(1, DIM, dtype=f32)],
        [pltpu.VMEM((DIM, DIM), bf16)] * 3 + [pltpu.VMEM((3, ROWS, DIM), bf16)] + sems(3),
        2 * 10**9,
        32,
        "input_back",
    )(*args)


def call_attention_weights_grad(*args):
    return call(
        attention_weights_grad,
        in_vmem(13),
        [shape(DIM, 2 * SHARE)] * 2,
        [
            pltpu.VMEM((SLOTS, 3 * SHARE), bf16),
            pltpu.VMEM((SLOTS, SHARE), bf16),
            pltpu.VMEM((DIM, SHARE), f32),
        ],
        2 * 10**9,
        40,
        "attention_weights_grad",
    )(*args)


def call_ffn_weights_grad(layer, groups, *args):
    quarter = FF // groups // 4
    parts = PARTS + 1
    scratch = [
        pltpu.VMEM((parts, DIM, FF_SHARE), bf16),
        pltpu.VMEM((parts, DIM, FF_SHARE), bf16),
        pltpu.VMEM((FF_SHARE, DIM), bf16),
    ]
    if layer == 1:
        scratch += [pltpu.VMEM((SLOTS, DIM), bf16)]
    scratch += [
        pltpu.VMEM((SLOTS, DIM), bf16),
        pltpu.VMEM((SLOTS, FF_SHARE), bf16),
        pltpu.VMEM((SLOTS, FF_SHARE), bf16),
        pltpu.VMEM((FF, SHARE), f32),
    ]
    return call(
        functools.partial(ffn_weights_grad, layer, groups),
        in_vmem(6 if layer == 0 else 8) + anywhere(6),
        [shape(DIM, FF_SHARE)] * 2 + [shape(groups * quarter, 2 * SHARE)] * 2,
        scratch + sems(11),
        5 * 10**9,
        48,
        "ffn_weights_grad",
    )(*args)


def rotary_tables():
    lanes = np.arange(128)
    frequency = (10000.0 ** (-2.0 * (lanes % 32) / HEAD_DIM)).astype(np.float32)
    angles = np.arange(SLOTS, dtype=np.float32)[:, None] * frequency[None, :]
    sign = np.where(lanes % HEAD_DIM < 32, -1.0, 1.0).astype(np.float32)
    return np.cos(angles).astype(np.float32), (np.sin(angles) * sign).astype(np.float32)


def swap(value):
    return lax.ppermute(value, "section", [(0, 1), (1, 0)])


def to_partner(value, offset):
    return lax.ppermute(value, "seq", [(part, part ^ offset) for part in range(PARTS)])


def gathered(value):
    return [value] + [to_partner(value, offset) for offset in range(1, PARTS)]


def exchanged(blocks):
    return [blocks[0]] + [to_partner(blocks[offset], offset) for offset in range(1, PARTS)]


def scatter_sum(keep, received):
    total = (keep.astype(f32) + received.astype(f32)).astype(bf16)
    return lax.psum_scatter(total, "dp", scatter_dimension=0, tiled=True)


def on_device(
    section_input, out_cotangent, lengths, attn_gain, w_query, w_key, w_value, w_output,
    ffn_gain, w_gate, w_up, w_down,
):
    groups = lax.axis_size("dp")
    core = lax.axis_index("section")
    is_first = core == 0
    inputs = lax.dynamic_index_in_dim(section_input, core, 0, keepdims=False)
    cotangent = lax.dynamic_index_in_dim(out_cotangent, core, 0, keepdims=False)
    length = lax.dynamic_slice_in_dim(lengths, core, 1, 0)
    cos, sin = (jnp.asarray(table) for table in rotary_tables())
    x_blocks = gathered(inputs)

    gains = jnp.concatenate([attn_gain, ffn_gain], axis=0).astype(f32)
    gains_pair = (gains, swap(gains))
    q_pair = (w_query, swap(w_query))
    k_pair = (w_key, swap(w_key))
    v_pair = (w_value, swap(w_value))
    o_pair = (w_output, swap(w_output))
    g_pair = (w_gate, swap(w_gate))
    u_pair = (w_up, swap(w_up))
    d_pair = (w_down, swap(w_down))
    qkv = q_pair + k_pair + v_pair
    ffn = g_pair + u_pair + d_pair

    normed_0, queries_0, keys_0, values_0, packed_0 = call_first_attention(
        *x_blocks, length, *gains_pair, cos, sin, *qkv
    )
    mixed_0 = gathered(packed_0)
    (after_0, normed_two_0, hidden_0, mid, normed_1, queries_1, keys_1, values_1, packed_1, *mixed_blocks) = (
        call_middle(*x_blocks, *mixed_0, length, *gains_pair, cos, sin, *o_pair, *ffn, *qkv)
    )
    mixed_rows = exchanged(mixed_blocks)
    output, normed_two_1, grad_after_1, gain_ffn_1, *grad_blocks_1 = call_last_rows(
        mid, cotangent, *mixed_rows, *gains_pair, *o_pair, *ffn
    )
    grad_mixed_1 = exchanged(grad_blocks_1)
    grad_qkv_1 = call_attention_back(*grad_mixed_1, length, cos, sin, queries_1, keys_1, values_1)
    grad_rows_1 = exchanged(grad_qkv_1)
    grad_mid, gain_attn_1 = call_input_back(1, *grad_rows_1, mid, grad_after_1, *gains_pair, *qkv)

    grad_after_0, gain_ffn_0, *grad_blocks_0 = call_first_rows_back(
        after_0, grad_mid, *gains_pair, *o_pair, *ffn
    )
    grad_mixed_0 = exchanged(grad_blocks_0)
    grad_qkv_0 = call_attention_back(*grad_mixed_0, length, cos, sin, queries_0, keys_0, values_0)
    grad_rows_0 = exchanged(grad_qkv_0)
    grad_first, gain_attn_0 = call_input_back(0, *grad_rows_0, inputs, grad_after_0, *gains_pair, *qkv)

    mixed_1 = gathered(packed_1)
    normed_two_all = gathered(normed_two_1)
    cotangent_all = gathered(cotangent)
    keep, send, keep_down, send_down = call_ffn_weights_grad(
        1, groups, *normed_two_all, *cotangent_all, *ffn
    )
    ffn_1 = (scatter_sum(keep, swap(send)), scatter_sum(keep_down, swap(send_down)))
    keep, send = call_attention_weights_grad(normed_1, *grad_qkv_1, *mixed_1, *grad_mixed_1)
    attn_1 = scatter_sum(keep, swap(send))

    grad_mid_all = gathered(grad_mid)
    keep, send, keep_down, send_down = call_ffn_weights_grad(
        0, groups, normed_two_0, hidden_0, *grad_mid_all, *ffn
    )
    ffn_0 = (scatter_sum(keep, swap(send)), scatter_sum(keep_down, swap(send_down)))
    keep, send = call_attention_weights_grad(normed_0, *grad_qkv_0, *mixed_0, *grad_mixed_0)
    attn_0 = scatter_sum(keep, swap(send))

    def sort(of_first, of_second):
        mine = jnp.where(is_first, of_first, of_second)
        other = swap(jnp.where(is_first, of_second, of_first))
        return jnp.where(is_first, mine, other), jnp.where(is_first, other, mine)

    section_outputs = jnp.stack(sort(mid, output))[None]
    input_grads = jnp.stack(sort(grad_first, grad_mid))[None]
    attn_low, attn_high = sort(attn_0, attn_1)
    gate, up = sort(ffn_0[0], ffn_1[0])
    down_low, down_high = sort(ffn_0[1], ffn_1[1])
    down = jnp.concatenate(
        [down_low[:, :SHARE], down_low[:, SHARE:], down_high[:, :SHARE], down_high[:, SHARE:]], axis=0
    )
    gains_0 = jnp.concatenate([gain_attn_0, gain_ffn_0], axis=0)
    gains_1 = jnp.concatenate([gain_attn_1, gain_ffn_1], axis=0)
    gain_total = jnp.where(is_first, gains_0, gains_1) + swap(jnp.where(is_first, gains_1, gains_0))
    gain_shares = lax.psum_scatter(gain_total, ("dp", "seq"), scatter_dimension=1, tiled=True)

    return (
        section_outputs,
        input_grads,
        gain_shares[0:1],
        attn_low[None, :, :SHARE].astype(f32),
        attn_low[None, :, SHARE:].astype(f32),
        attn_high[None, :, :SHARE].astype(f32),
        attn_high[None, :, SHARE:].astype(f32),
        gain_shares[1:2],
        gate[None].astype(f32),
        up[None].astype(f32),
        down[None].astype(f32),
    )


def solution(mesh):
    return jax.shard_map(
        on_device,
        mesh=mesh,
        in_specs=(
            P("dp", "seq", None),
            P("dp", "seq", None),
            P("dp"),
            P("section", None),
            P("section", None, None),
            P("section", None, None),
            P("section", None, None),
            P("section", None, None),
            P("section", None),
            P("section", None, None),
            P("section", None, None),
            P("section", None, None),
        ),
        out_specs=(
            P("section", "dp", "seq", None),
            P("section", "dp", "seq", None),
            P("section", ("dp", "seq")),
            P("section", "dp", "seq"),
            P("section", "dp", "seq"),
            P("section", "dp", "seq"),
            P("section", "dp", "seq"),
            P("section", ("dp", "seq")),
            P("section", "dp", "seq"),
            P("section", "dp", "seq"),
            P("section", "dp", "seq"),
        ),
        check_vma=False,
    )
```

```python
import functools

import jax
import jax.numpy as jnp
import numpy as np
from jax import lax
from jax.experimental import pallas as pl
from jax.experimental.pallas import tpu as pltpu
from jax.sharding import PartitionSpec as P

DIM = 768
HEAD_DIM = 64
FF = 2048
ROWS = 160
PARTS = 4
SLOTS = ROWS * PARTS
SHARE_HEADS = 3
SHARE = SHARE_HEADS * HEAD_DIM
FF_SHARE = FF // PARTS
PACKED = SLOTS * 3 // 2
PACKED_ROWS = ROWS * 3 // 2
WINDOW = 256
QUERY_BLOCKS = ((0, 256), (256, 256), (512, 128))
HALVES = ((0, 320), (320, 320))

epsilon = 1e-05
masked_score = -1e30
bf16 = jnp.bfloat16
f32 = jnp.float32
MIB = 1 << 20
VMEM_MIB = 60
GAIN_ROWS = 16
COST = 10**9


def nn(left, right):
    return lax.dot_general(left, right, (((1,), (0,)), ((), ())), preferred_element_type=f32)


def nt(left, right):
    return lax.dot_general(left, right, (((1,), (1,)), ((), ())), preferred_element_type=f32)


def tn(left, right):
    return lax.dot_general(left, right, (((0,), (0,)), ((), ())), preferred_element_type=f32)


def rms_scale(values):
    return lax.rsqrt(jnp.mean(values * values, axis=-1, keepdims=True) + epsilon)


def rotate(values, cosine, signed_sine):
    width = values.shape[-1]
    lane = lax.broadcasted_iota(jnp.int32, values.shape, 1)
    ahead = pltpu.roll(values, width - 32, 1)
    behind = pltpu.roll(values, 32, 1)
    partner = jnp.where(lane % HEAD_DIM < 32, ahead, behind)
    return values * cosine + partner * signed_sine


def wide(table):
    return jnp.concatenate([table, table], axis=1)


def unpack(packed, count):
    tail = packed[count:]
    third = jnp.concatenate([tail[:, :HEAD_DIM], tail[:, HEAD_DIM:]], axis=0)
    return jnp.concatenate([packed[:count], third], axis=1)


def gain_row(gains, kind):
    rows = gains[...].astype(f32)
    return jnp.concatenate([rows[3 * kind + part : 3 * kind + part + 1, :] for part in range(3)], axis=1)


def place():
    return lax.axis_index("section"), lax.axis_index("seq")


def block_rows(index, size=ROWS):
    return pl.ds(pl.multiple_of(index * size, size), size)


def window_start(seq):
    return pl.multiple_of(((3 * seq) >> 1) * 128, 128)


class Mover:
    def __init__(self, sems, core=None):
        self.sems = sems
        self.core = core
        self.count = 0
        self.sent = []

    def next_sem(self):
        self.count += 1
        return self.sems.at[self.count - 1]

    def fetch(self, source, target):
        copy = pltpu.make_async_copy(source, target, self.next_sem())
        copy.start()
        return copy

    def fetch_all(self, sources, targets):
        return [self.fetch(source, target) for source, target in zip(sources, targets)]

    def fetch_layer(self, layer, own, other, target):
        sem = self.next_sem()

        @pl.when(self.core == layer)
        def _():
            pltpu.make_async_copy(own, target, sem).start()

        @pl.when(self.core != layer)
        def _():
            pltpu.make_async_copy(other, target, sem).start()

        return pltpu.make_async_copy(own, target, sem)

    def fetch_windows(self, layer, pair, targets):
        return [
            self.fetch_layer(layer, pair[0].at[block_rows(kind, DIM), :], pair[1].at[block_rows(kind, DIM), :], target)
            for kind, target in enumerate(targets)
        ]

    def fetch_gains(self, layer, pair, target):
        rows = slice(3 * DIM, 3 * DIM + GAIN_ROWS)
        return self.fetch_layer(layer, pair[0].at[rows, :], pair[1].at[rows, :], target)

    def fetch_ffn(self, layer, pairs, targets):
        copies = []
        for part in range(PARTS):
            span = slice(part * FF_SHARE, (part + 1) * FF_SHARE)
            (g_own, g_other), (u_own, u_other), (d_own, d_other) = pairs
            copies.append(
                (
                    self.fetch_layer(layer, g_own.at[0, :, span], g_other.at[0, :, span], targets[0].at[part]),
                    self.fetch_layer(layer, u_own.at[0, :, span], u_other.at[0, :, span], targets[1].at[part]),
                    self.fetch_layer(layer, d_own.at[0, span, :], d_other.at[0, span, :], targets[2].at[span, :]),
                )
            )
        return copies

    def send(self, source, target):
        copy = pltpu.make_async_copy(source, target, self.next_sem())
        copy.start()
        self.sent.append(copy)

    def finish(self):
        for copy in self.sent:
            copy.wait()


def wait(copies):
    for copy in copies:
        copy.wait()


def project(normed, windows, odd, cos, sin, heads, value_t):
    for first, count in QUERY_BLOCKS:
        rows = slice(first, first + count)
        block = normed[rows, :]
        cosine, sine = wide(cos[rows, :]), wide(sin[rows, :])
        for kind, window in enumerate(windows):
            result = nn(block, window[...])
            if kind < 2:
                result = rotate(result, cosine, sine)
            if kind == 0:
                result = result * HEAD_DIM ** (-0.5)
            result = jnp.where(odd, pltpu.roll(result, WINDOW - HEAD_DIM, 1), result)
            low = result.astype(bf16)
            for head in range(SHARE_HEADS):
                heads[kind, head, rows, :] = low[:, head * HEAD_DIM : (head + 1) * HEAD_DIM]
            if kind == 2:
                turned = jnp.transpose(result).astype(bf16)
                for head in range(SHARE_HEADS):
                    value_t[head, :, rows] = turned[head * HEAD_DIM : (head + 1) * HEAD_DIM, :]


def masked(scores_t, first, length):
    spots = lax.broadcasted_iota(jnp.int32, scores_t.shape, 0)
    query = first + lax.broadcasted_iota(jnp.int32, (1, scores_t.shape[1]), 1)
    bound = jnp.minimum(query + 1, length)
    return jnp.where(spots < bound, scores_t, masked_score)


def attend(heads, value_t, length, mixed_t):
    for head in range(SHARE_HEADS):
        for first, count in QUERY_BLOCKS:
            last = first + count
            scores = nt(heads[1, head, :last, :], heads[0, head, first:last, :])
            scores = masked(scores, first, length)
            exponent = jnp.exp(scores - jnp.max(scores, axis=0, keepdims=True))
            total = jnp.sum(exponent, axis=0, keepdims=True)
            mixed = nn(value_t[head, :, :last], exponent.astype(bf16))
            mixed_t[head, :, first:last] = mixed * (1.0 / total)


def untranspose(mixed_t, pair, single):
    both = jnp.concatenate([mixed_t[0], mixed_t[1]], axis=0)
    pair[...] = jnp.transpose(both).astype(bf16)
    last = jnp.concatenate([mixed_t[2], mixed_t[2]], axis=0)
    single[...] = jnp.transpose(last).astype(bf16)


def pack_all(pair, single, target):
    half = SLOTS // 2
    target[:SLOTS, :] = pair[...]
    target[SLOTS:, :] = jnp.concatenate(
        [single[:half, :HEAD_DIM], single[half:, :HEAD_DIM]], axis=1
    )


def pack_block(pair, single, index, target):
    half = ROWS // 2
    rows = block_rows(index)
    target[:ROWS, :] = pair[rows, :]
    tail = single[rows, :]
    target[ROWS:, :] = jnp.concatenate([tail[:half, :HEAD_DIM], tail[half:, :HEAD_DIM]], axis=1)


def columns_of(array, first, rows=slice(None)):
    return array[rows, first * 128 : (first + 1) * 128]


def norm_back(grad_normed, gain, normed, scale):
    scaled = grad_normed * gain
    return scale * (scaled - normed * jnp.mean(scaled * normed, axis=-1, keepdims=True))


def ffn_back_chunk(gate, up, grad_hidden):
    sigmoid = jax.nn.sigmoid(gate)
    grad_gate = grad_hidden * up * sigmoid * (1.0 + gate * (1.0 - sigmoid))
    grad_up = grad_hidden * gate * sigmoid
    return grad_gate.astype(bf16), grad_up.astype(bf16)


def pack_windows(seq_weights_h, gains_h, packed_h, packed, gains, sems):
    _, seq = place()
    move = Mover(sems)
    span = pl.ds(window_start(seq), WINDOW)
    copies = move.fetch_all(gains_h, gains)
    copies += [
        move.fetch(weight.at[0, :, span], packed.at[block_rows(kind, DIM), :])
        for kind, weight in enumerate(seq_weights_h)
    ]
    wait(copies)
    rows = [gain[:, part * WINDOW : (part + 1) * WINDOW].astype(f32) for gain in gains for part in range(3)]
    rows.append(jnp.zeros((GAIN_ROWS - 6, WINDOW), f32))
    packed[3 * DIM :, :] = jnp.concatenate(rows, axis=0).astype(bf16)
    move.send(packed, packed_h)
    move.finish()


def first_attention(
    x_h, lengths, cos_h, sin_h, windows_h,
    normed_h, heads_h, packed_h,
    x_blocks, gains, cos, sin, windows, normed, heads, packed, value_t, mixed_t, pair, single, sems,
):
    core, seq = place()
    move = Mover(sems, core)
    copies_x = move.fetch_all(x_h, x_blocks)
    copy_gains = move.fetch_gains(0, windows_h, gains)
    copies_qkv = move.fetch_windows(0, windows_h, windows)
    copies_table = move.fetch_all((cos_h, sin_h), (cos, sin))
    copy_gains.wait()
    gain = gain_row(gains, 0)
    for offset, block in enumerate(x_blocks):
        copies_x[offset].wait()
        wide_block = block[...].astype(f32)
        normed[block_rows(seq ^ offset), :] = (wide_block * rms_scale(wide_block) * gain).astype(bf16)
    move.send(normed, normed_h)
    wait(copies_table + copies_qkv)
    project(normed, windows, seq % 2 == 1, cos, sin, heads, value_t)
    move.send(heads, heads_h)
    attend(heads, value_t, lengths[core], mixed_t)
    untranspose(mixed_t, pair, single)
    pack_all(pair, single, packed)
    move.send(packed, packed_h)
    move.finish()


def middle(
    x_h, mixed_h, lengths, cos_h, sin_h, o_h, ffn_h, windows_h,
    after_h, normed_two_h, hidden_h, mid_h, normed_h, heads_h, packed_h, blocks_h,
    x_blocks, mixed, gains, gains_next, cos, sin, w_o, w_g, w_u, w_d, windows,
    after, normed_two, hidden, mid, normed, heads, packed, blocks, total, value_t, mixed_t, pair, single, sems,
):
    core, seq = place()
    move = Mover(sems, core)
    copies_x = move.fetch_all(x_h, x_blocks)
    copy_o = move.fetch_layer(0, o_h[0].at[0], o_h[1].at[0], w_o)
    copies_gain = [move.fetch_gains(0, windows_h, gains), move.fetch_gains(1, windows_h, gains_next)]
    copies_mixed = move.fetch_all(mixed_h, mixed)
    copies_ffn = move.fetch_ffn(0, ffn_h, (w_g, w_u, w_d))
    copies_qkv = move.fetch_windows(1, windows_h, windows)
    copies_table = move.fetch_all((cos_h, sin_h), (cos, sin))
    for offset, block in enumerate(x_blocks):
        copies_x[offset].wait()
        after[block_rows(seq ^ offset), :] = block[...].astype(f32)
    copy_o.wait()
    for offset, block in enumerate(mixed):
        share = w_o[block_rows(seq ^ offset, SHARE), :]
        copies_mixed[offset].wait()
        whole = unpack(block[...], SLOTS)
        for first, count in HALVES:
            rows = slice(first, first + count)
            after[rows, :] += nn(whole[rows], share)
    wait(copies_gain)
    gain_ffn = gain_row(gains, 1)
    gain_attn = gain_row(gains_next, 0)
    for first, count in HALVES:
        rows = slice(first, first + count)
        block = after[rows, :]
        normed_two[rows, :] = (block * rms_scale(block) * gain_ffn).astype(bf16)
        total[rows, :] = block
    move.send(after.at[block_rows(seq), :], after_h)
    move.send(normed_two, normed_two_h)
    for part in range(PARTS):
        wait(copies_ffn[part])
        span = slice(part * FF_SHARE, (part + 1) * FF_SHARE)
        for first, count in HALVES:
            rows = slice(first, first + count)
            block = normed_two[rows, :]
            gate = nn(block, w_g[part])
            up = nn(block, w_u[part])
            low = (gate * jax.nn.sigmoid(gate) * up).astype(bf16)
            hidden[rows, span] = low
            total[rows, :] += nn(low, w_d[span, :])
    move.send(hidden, hidden_h)
    for first, count in HALVES:
        rows = slice(first, first + count)
        low = total[rows, :].astype(bf16)
        mid[rows, :] = low
        block = low.astype(f32)
        normed[rows, :] = (block * rms_scale(block) * gain_attn).astype(bf16)
    move.send(mid.at[block_rows(seq), :], mid_h)
    move.send(normed, normed_h)
    wait(copies_table + copies_qkv)
    project(normed, windows, seq % 2 == 1, cos, sin, heads, value_t)
    move.send(heads, heads_h)
    attend(heads, value_t, lengths[core], mixed_t)
    untranspose(mixed_t, pair, single)
    for offset, (block, target) in enumerate(zip(blocks, blocks_h)):
        pack_block(pair, single, seq ^ offset, block)
        move.send(block, target)
    pack_all(pair, single, packed)
    move.send(packed, packed_h)
    move.finish()


def send_blocks(move, seq, grad_branch, w_o, blocks, blocks_h):
    for here in range(PARTS):

        @pl.when(seq == here)
        def _():
            for offset, block in enumerate(blocks):
                other = here ^ offset
                span = slice(other * SHARE, (other + 1) * SHARE)
                grad_heads = nt(grad_branch[...], w_o[span, :]).astype(bf16)
                block[...] = jnp.concatenate([grad_heads, grad_branch[:, span]], axis=1)

    for block, target in zip(blocks, blocks_h):
        move.send(block, target)


def last_rows(
    mid_h, cotangent_h, mixed_h, windows_h, o_h, ffn_h,
    output_h, normed_two_h, grad_after_h, grad_gain_h, blocks_h,
    mid, cotangent, mixed, gains, w_o, w_g, w_u, w_d,
    output, normed_two, grad_after, grad_gain, blocks, branch, hidden, sems,
):
    core, seq = place()
    move = Mover(sems, core)
    copies = move.fetch_all((mid_h, cotangent_h.at[core]), (mid, cotangent))
    copies.append(move.fetch_gains(1, windows_h, gains))
    copy_o = move.fetch_layer(1, o_h[0].at[0], o_h[1].at[0], w_o)
    copies_mixed = move.fetch_all(mixed_h, mixed)
    copies_ffn = move.fetch_ffn(1, ffn_h, (w_g, w_u, w_d))
    wait(copies)
    gain = gain_row(gains, 1)
    copy_o.wait()
    after = mid[...].astype(f32)
    for offset, block in enumerate(mixed):
        copies_mixed[offset].wait()
        after = after + nn(unpack(block[...], ROWS), w_o[block_rows(seq ^ offset, SHARE), :])
    scale = rms_scale(after)
    normed = after * scale
    low = (normed * gain).astype(bf16)
    normed_two[...] = low
    move.send(normed_two, normed_two_h)
    grad_low = cotangent[...]
    grad_normed = jnp.zeros((ROWS, DIM), f32)
    for part in range(PARTS):
        wait(copies_ffn[part])
        gate = nn(low, w_g[part])
        up = nn(low, w_u[part])
        span = slice(part * FF_SHARE, (part + 1) * FF_SHARE)
        hidden[:, span] = (gate * jax.nn.sigmoid(gate) * up).astype(bf16)
        grad_gate, grad_up = ffn_back_chunk(gate, up, nt(grad_low, w_d[span, :]))
        grad_normed = grad_normed + nt(grad_gate, w_g[part]) + nt(grad_up, w_u[part])
    grad_gain[...] = jnp.sum(grad_normed * normed, axis=0, keepdims=True)
    move.send(grad_gain, grad_gain_h)
    total = grad_low.astype(f32) + norm_back(grad_normed, gain, normed, scale)
    grad_after[...] = total
    move.send(grad_after, grad_after_h)
    branch[...] = total.astype(bf16)
    send_blocks(move, seq, branch, w_o, blocks, blocks_h)
    output[...] = (after + nn(hidden[...], w_d[...])).astype(bf16)
    move.send(output, output_h)
    move.finish()


def first_rows_back(
    after_h, grad_in_h, windows_h, o_h, ffn_h,
    grad_after_h, grad_gain_h, blocks_h,
    after_own, grad_in, gains, w_o, w_g, w_u, w_d, grad_after, grad_gain, blocks, branch, sems,
):
    core, seq = place()
    move = Mover(sems, core)
    copies = move.fetch_all((after_h, grad_in_h), (after_own, grad_in))
    copies.append(move.fetch_gains(0, windows_h, gains))
    copies_ffn = move.fetch_ffn(0, ffn_h, (w_g, w_u, w_d))
    copy_o = move.fetch_layer(0, o_h[0].at[0], o_h[1].at[0], w_o)
    wait(copies)
    gain = gain_row(gains, 1)
    after = after_own[...]
    scale = rms_scale(after)
    normed = after * scale
    low = (normed * gain).astype(bf16)
    grad_low = grad_in[...]
    grad_normed = jnp.zeros((ROWS, DIM), f32)
    for part in range(PARTS):
        wait(copies_ffn[part])
        gate = nn(low, w_g[part])
        up = nn(low, w_u[part])
        span = slice(part * FF_SHARE, (part + 1) * FF_SHARE)
        grad_gate, grad_up = ffn_back_chunk(gate, up, nt(grad_low, w_d[span, :]))
        grad_normed = grad_normed + nt(grad_gate, w_g[part]) + nt(grad_up, w_u[part])
    grad_gain[...] = jnp.sum(grad_normed * normed, axis=0, keepdims=True)
    move.send(grad_gain, grad_gain_h)
    total = grad_low.astype(f32) + norm_back(grad_normed, gain, normed, scale)
    grad_after[...] = total
    move.send(grad_after, grad_after_h)
    branch[...] = total.astype(bf16)
    copy_o.wait()
    send_blocks(move, seq, branch, w_o, blocks, blocks_h)
    move.finish()


def attention_back(
    grads_h, lengths, cos_h, sin_h, heads_h,
    blocks_h,
    grads, cos, sin, heads, grad_mixed, key_t, query_grad_t, key_grad, value_grad, whole, sems,
):
    core, seq = place()
    move = Mover(sems)
    copies_grads = move.fetch_all(grads_h, grads)
    copy_heads = move.fetch(heads_h, heads)
    copies_table = move.fetch_all((cos_h, sin_h), (cos, sin))
    key_grad[...] = jnp.zeros_like(key_grad)
    value_grad[...] = jnp.zeros_like(value_grad)
    for offset, block in enumerate(grads):
        copies_grads[offset].wait()
        low = block[:, :SHARE]
        for head in range(SHARE_HEADS):
            grad_mixed[head, block_rows(seq ^ offset), :] = low[:, head * HEAD_DIM : (head + 1) * HEAD_DIM]
    copy_heads.wait()
    length = lengths[core]

    for head in range(SHARE_HEADS):
        key_wide = heads[1, head].astype(f32)
        key_t[...] = jnp.transpose(jnp.concatenate([key_wide, key_wide], axis=1))[:HEAD_DIM].astype(bf16)
        for first, count in QUERY_BLOCKS:
            last = first + count
            query = heads[0, head, first:last, :]
            grad = grad_mixed[head, first:last, :]
            scores = nt(heads[1, head, :last, :], query)
            scores = masked(scores, first, length)
            exponent = jnp.exp(scores - jnp.max(scores, axis=0, keepdims=True))
            weights = exponent * (1.0 / jnp.sum(exponent, axis=0, keepdims=True))
            grad_weights = nt(heads[2, head, :last, :], grad)
            row_total = jnp.sum(weights * grad_weights, axis=0, keepdims=True)
            grad_scores = (weights * (grad_weights - row_total)).astype(bf16)
            value_grad[head, :last, :] += nn(weights.astype(bf16), grad)
            key_grad[head, :last, :] += nn(grad_scores, query)
            query_grad_t[head, :, first:last] = nn(key_t[:, :last], grad_scores) * HEAD_DIM ** (-0.5)

    turned = jnp.concatenate([query_grad_t[0], query_grad_t[1], query_grad_t[2], query_grad_t[2]], axis=0)
    query_side = jnp.transpose(turned)
    key_side = jnp.concatenate([key_grad[0], key_grad[1], key_grad[2], key_grad[2]], axis=1)
    value_side = jnp.concatenate([value_grad[0], value_grad[1], value_grad[2]], axis=1)
    wait(copies_table)
    cosine, sine = wide(cos[...]), wide(sin[...])
    query_side = rotate(query_side, cosine, -sine)[:, :SHARE]
    key_side = rotate(key_side, cosine, -sine)[:, :SHARE]
    whole[...] = jnp.concatenate([query_side, key_side, value_side], axis=1).astype(bf16)
    for offset, target in enumerate(blocks_h):
        move.send(whole.at[block_rows(seq ^ offset), :], target)
    move.finish()


def input_back(
    layer, blocks_h, inputs_h, grad_after_h, windows_h, qkv_h,
    grad_in_h, grad_gain_h,
    blocks, inputs, grad_after, gains, weights, grad_in, grad_gain, sides, sems,
):
    core, seq = place()
    move = Mover(sems, core)
    copies_blocks = move.fetch_all(blocks_h, blocks)
    copies = move.fetch_all((inputs_h, grad_after_h), (inputs, grad_after))
    copies.append(move.fetch_gains(layer, windows_h, gains))
    copies_qkv = [
        move.fetch_layer(layer, own.at[0], other.at[0], target) for (own, other), target in zip(qkv_h, weights)
    ]
    wait(copies_blocks)
    for here in range(PARTS):

        @pl.when(seq == here)
        def _():
            for kind in range(3):
                span = slice(kind * SHARE, (kind + 1) * SHARE)
                sides[kind] = jnp.concatenate(
                    [blocks[here ^ part][:, span] for part in range(PARTS)], axis=1
                )

    wait(copies)
    gain = gain_row(gains, 0)
    wide_inputs = inputs[...].astype(f32)
    scale = rms_scale(wide_inputs)
    normed = wide_inputs * scale
    grad_normed = jnp.zeros((ROWS, DIM), f32)
    for kind, weight in enumerate(weights):
        copies_qkv[kind].wait()
        grad_normed = grad_normed + nt(sides[kind], weight[...])
    grad_in[...] = (grad_after[...] + norm_back(grad_normed, gain, normed, scale)).astype(bf16)
    move.send(grad_in, grad_in_h)
    grad_gain[...] = jnp.sum(grad_normed * normed, axis=0, keepdims=True)
    move.send(grad_gain, grad_gain_h)
    move.finish()


def attention_weights_grad(
    normed_h, blocks_h, mixed_h, grads_h,
    result_h,
    normed, blocks, mixed, grads, packed, whole, branch, output_grad, sems,
):
    _, seq = place()
    move = Mover(sems)
    copies = move.fetch_all(mixed_h, mixed)
    copies += move.fetch_all(grads_h, grads)
    copies_qkv = move.fetch_all(blocks_h, blocks) + [move.fetch(normed_h, normed)]
    wait(copies)
    for offset, grad in enumerate(grads):
        branch[block_rows(seq ^ offset), :] = grad[:, SHARE:]
    for offset, block in enumerate(mixed):
        output_grad[block_rows(seq ^ offset, SHARE), :] = tn(unpack(block[...], SLOTS), branch[...])
    wait(copies_qkv)
    for offset, block in enumerate(blocks):
        whole[block_rows(seq ^ offset), :] = block[...]
    result = tn(normed[...], whole[...])
    last = jnp.concatenate([result[:, 2 * SHARE :], output_grad[...]], axis=1)
    rows = DIM // packed.shape[0]
    for group in range(packed.shape[0]):
        span = slice(group * rows, (group + 1) * rows)
        for tile in range(6):
            source = columns_of((result, last)[tile // 3], tile % 3, span)
            packed[group, tile * rows : (tile + 1) * rows, :] = source.astype(bf16)
    move.send(packed, result_h)
    move.finish()


def ffn_weights_grad(
    layer, left_h, y_h, ffn_h,
    result_h,
    packed, w_g, w_u, w_d, normed_two, hidden, grad_out, grad_gate, grad_up, down, sems,
):
    core, seq = place()
    move = Mover(sems, core)
    (g_own, g_other), (u_own, u_other), (d_own, d_other) = ffn_h
    span = pl.ds(pl.multiple_of(seq * FF_SHARE, FF_SHARE), FF_SHARE)
    if layer == 0:
        copies = move.fetch_all(left_h, (normed_two, hidden))
        copies += [move.fetch(block, grad_out.at[block_rows(seq ^ offset), :]) for offset, block in enumerate(y_h)]
    else:
        copies = [move.fetch(block, normed_two.at[block_rows(seq ^ offset), :]) for offset, block in enumerate(left_h)]
        copies += [
            move.fetch(y_h.at[part, core], grad_out.at[part * ROWS : (part + 1) * ROWS, :]) for part in range(PARTS)
        ]
    copies += [
        move.fetch_layer(layer, g_own.at[0, :, span], g_other.at[0, :, span], w_g.at[PARTS]),
        move.fetch_layer(layer, u_own.at[0, :, span], u_other.at[0, :, span], w_u.at[PARTS]),
        move.fetch_layer(layer, d_own.at[0, span, :], d_other.at[0, span, :], w_d),
    ]
    copies_ffn = []
    if layer == 1:
        for part in range(PARTS):
            part_span = slice(part * FF_SHARE, (part + 1) * FF_SHARE)
            copies_ffn.append(
                (
                    move.fetch_layer(layer, g_own.at[0, :, part_span], g_other.at[0, :, part_span], w_g.at[part]),
                    move.fetch_layer(layer, u_own.at[0, :, part_span], u_other.at[0, :, part_span], w_u.at[part]),
                )
            )
    wait(copies)
    for first, count in HALVES:
        rows = slice(first, first + count)
        block = normed_two[rows, :]
        grad_gate[rows, :], grad_up[rows, :] = ffn_back_chunk(
            nn(block, w_g[PARTS]), nn(block, w_u[PARTS]), nt(grad_out[rows, :], w_d[...])
        )
    groups = packed.shape[0]
    tile_rows = DIM // groups
    for index, grads in enumerate((grad_gate, grad_up)):
        result = tn(normed_two[...], grads[...])
        for group in range(groups):
            span = slice(group * tile_rows, (group + 1) * tile_rows)
            for tile in range(4):
                packed[group, index, tile * tile_rows : (tile + 1) * tile_rows, :] = columns_of(result, tile, span).astype(bf16)

    window = grad_out[:, pl.ds(window_start(seq), WINDOW)].astype(f32)
    columns = jnp.where(seq % 2 == 1, pltpu.roll(window, WINDOW - HEAD_DIM, 1), window)
    columns = columns[:, :SHARE].astype(bf16)
    for part in range(PARTS):
        part_span = slice(part * FF_SHARE, (part + 1) * FF_SHARE)
        if layer == 1:
            wait(copies_ffn[part])
            for first, count in HALVES:
                rows = slice(first, first + count)
                gate = nn(normed_two[rows, :], w_g[part])
                up = nn(normed_two[rows, :], w_u[part])
                hidden[rows, part_span] = (gate * jax.nn.sigmoid(gate) * up).astype(bf16)
        down[part_span, :] = tn(hidden[:, part_span], columns)
    quarter = FF // groups // 4
    for index in range(2):
        for group in range(groups):
            begin = (group * 4 + index * 2) * quarter
            both = jnp.concatenate(
                [down[begin : begin + quarter, :], down[begin + quarter : begin + 2 * quarter, :]], axis=1
            ).astype(bf16)
            for tile in range(3):
                place_at = 4 * tile_rows + tile * quarter
                packed[group, index, place_at : place_at + quarter, :] = columns_of(both, tile)
    move.send(packed, result_h)
    move.finish()


def join_attention(parts_h, gains_h, result_h, gains, result, sems):
    move = Mover(sems)
    rows = result.shape[2] - GAIN_ROWS
    copies = [move.fetch(part, result.at[:, layer, :rows, :]) for layer, part in enumerate(parts_h)]
    move.fetch(gains_h, gains).wait()
    result[:, :, rows:, :] = gains[...].astype(bf16)
    wait(copies)
    move.send(result, result_h)
    move.finish()


def write_weights(
    ffn_0, ffn_1, attn_h, ffn_other_0, ffn_other_1,
    q_h, k_h, v_h, o_h, g_h, u_h, d_h, gain_h,
    ffn_low, ffn_high, attn, q, k, v, o, g, u, d, gain, sems,
):
    core, _ = place()
    move = Mover(sems, core)
    copies = [
        move.fetch_layer(0, ffn_0, ffn_other_1, ffn_low),
        move.fetch_layer(0, ffn_other_0, ffn_1, ffn_high),
        move.fetch(attn_h, attn),
    ]
    wait(copies)
    rows = q.shape[1]
    quarter = d.shape[2] // 4
    for index, (ffn, wide_out, pair) in enumerate(((ffn_low, g, (q, k)), (ffn_high, u, (v, o)))):
        for tile in range(4):
            wide_out[0, :, tile * 128 : (tile + 1) * 128] = ffn[tile * rows : (tile + 1) * rows, :].astype(f32)
        place_at = 4 * rows
        both = jnp.concatenate(
            [ffn[place_at + tile * quarter : place_at + (tile + 1) * quarter, :].astype(f32) for tile in range(3)],
            axis=1,
        )
        begin = index * 2 * quarter
        turned = jnp.transpose(both)
        d[0, :, begin : begin + quarter] = turned[:SHARE]
        d[0, :, begin + quarter : begin + 2 * quarter] = turned[SHARE:]
        both = jnp.concatenate(
            [
                attn[(index * 3 + tile) * rows : (index * 3 + tile + 1) * rows, :].astype(f32)
                for tile in range(3)
            ],
            axis=1,
        )
        pair[0][0] = both[:, :SHARE]
        pair[1][0] = both[:, SHARE:]
    for source, target in zip((q, k, v, o, g, u, d), (q_h, k_h, v_h, o_h, g_h, u_h, d_h)):
        move.send(source, target)
    gain[...] = attn[6 * rows :, :].astype(f32)
    move.send(gain, gain_h)
    move.finish()


def shape(*dims, dtype=bf16):
    return jax.ShapeDtypeStruct(dims, dtype)


def vm(*dims, dtype=bf16):
    return pltpu.VMEM(dims, dtype)


def call(body, args, outs, scratch, micros, name, after=()):
    leaves, tree = jax.tree.flatten(args)
    out_leaves, out_tree = jax.tree.flatten(outs)
    scratch_leaves, scratch_tree = jax.tree.flatten(scratch)
    count_in, count_all = len(leaves), len(leaves) + len(after)

    def kernel(*refs):
        ins = jax.tree.unflatten(tree, refs[:count_in])
        results = jax.tree.unflatten(out_tree, refs[count_all : count_all + len(out_leaves)])
        temps = jax.tree.unflatten(scratch_tree, refs[count_all + len(out_leaves) :])
        body(*ins, *results, *temps)

    def spec(leaf):
        small = leaf.dtype == jnp.int32
        return pl.BlockSpec(memory_space=pltpu.SMEM if small else pltpu.HBM)

    results = pl.pallas_call(
        kernel,
        out_shape=out_leaves,
        in_specs=[spec(leaf) for leaf in leaves] + [pl.BlockSpec(memory_space=pltpu.HBM)] * len(after),
        out_specs=[pl.BlockSpec(memory_space=pltpu.HBM)] * len(out_leaves),
        scratch_shapes=scratch_leaves,
        compiler_params=pltpu.CompilerParams(vmem_limit_bytes=VMEM_MIB * MIB),
        cost_estimate=pl.CostEstimate(flops=micros * COST, bytes_accessed=10**4, transcendentals=0),
        name=name,
    )(*leaves, *after)
    return jax.tree.unflatten(out_tree, results)


def sems(count):
    return pltpu.SemaphoreType.DMA((count,))


GAINS = vm(GAIN_ROWS, WINDOW)
TABLES = [vm(SLOTS, 128, dtype=f32)] * 2
HEADS = (3, SHARE_HEADS, SLOTS, HEAD_DIM)
WEIGHTS = [vm(DIM, DIM), vm(PARTS, DIM, FF_SHARE), vm(PARTS, DIM, FF_SHARE), vm(FF, DIM)]
ATTEND = [
    vm(SHARE_HEADS, HEAD_DIM, SLOTS),
    vm(SHARE_HEADS, HEAD_DIM, SLOTS, dtype=f32),
    vm(SLOTS, 128),
    vm(SLOTS, 128),
]
WINDOWS = [vm(DIM, WINDOW)] * 3
ROW = (ROWS, DIM)
BRANCH = (ROWS, 2 * SHARE)
QKV = (ROWS, 3 * SHARE)


def call_pack_windows(weights, gains):
    rows = 3 * DIM + GAIN_ROWS
    return call(
        pack_windows,
        (weights, gains),
        [shape(rows, WINDOW)],
        [vm(rows, WINDOW), [vm(1, DIM)] * 2, sems(8)],
        3,
        "pack_windows",
    )[0]


def call_first_attention(*args):
    return call(
        first_attention,
        args,
        [shape(SLOTS, DIM), shape(*HEADS), shape(PACKED, 128)],
        [[vm(*ROW)] * 4, GAINS, *TABLES, WINDOWS, vm(SLOTS, DIM), vm(*HEADS), vm(PACKED, 128), *ATTEND, sems(16)],
        10,
        "first_attention",
    )


def call_middle(*args):
    return call(
        middle,
        args,
        [
            shape(*ROW, dtype=f32), shape(SLOTS, DIM), shape(SLOTS, FF), shape(*ROW), shape(SLOTS, DIM),
            shape(*HEADS), shape(PACKED, 128), [shape(PACKED_ROWS, 128)] * 4,
        ],
        [
            [vm(*ROW)] * 4, [vm(PACKED, 128)] * 4, GAINS, GAINS, *TABLES, *WEIGHTS, WINDOWS,
            vm(SLOTS, DIM, dtype=f32), vm(SLOTS, DIM), vm(SLOTS, FF), vm(SLOTS, DIM), vm(SLOTS, DIM),
            vm(*HEADS), vm(PACKED, 128), [vm(PACKED_ROWS, 128)] * 4, vm(SLOTS, DIM, dtype=f32), *ATTEND, sems(48),
        ],
        20,
        "middle",
    )


def call_last_rows(*args, after=()):
    return call(
        last_rows,
        args,
        [shape(*ROW), shape(*ROW), shape(*ROW, dtype=f32), shape(1, DIM, dtype=f32), [shape(*BRANCH)] * 4],
        [
            vm(*ROW), vm(*ROW), [vm(PACKED_ROWS, 128)] * 4, GAINS, *WEIGHTS,
            vm(*ROW), vm(*ROW), vm(*ROW, dtype=f32), vm(1, DIM, dtype=f32), [vm(*BRANCH)] * 4,
            vm(*ROW), vm(ROWS, FF), sems(32),
        ],
        11,
        "last_rows",
        after,
    )


def call_first_rows_back(*args, after=()):
    return call(
        first_rows_back,
        args,
        [shape(*ROW, dtype=f32), shape(1, DIM, dtype=f32), [shape(*BRANCH)] * 4],
        [
            vm(*ROW, dtype=f32), vm(*ROW), GAINS, *WEIGHTS,
            vm(*ROW, dtype=f32), vm(1, DIM, dtype=f32), [vm(*BRANCH)] * 4, vm(*ROW), sems(32),
        ],
        10,
        "first_rows_back",
        after,
    )


def call_attention_back(*args, after=()):
    return call(
        attention_back,
        args,
        [[shape(*QKV)] * 4],
        [
            [vm(*BRANCH)] * 4, *TABLES, vm(*HEADS), vm(SHARE_HEADS, SLOTS, HEAD_DIM), vm(HEAD_DIM, SLOTS),
            vm(SHARE_HEADS, HEAD_DIM, SLOTS, dtype=f32), vm(SHARE_HEADS, SLOTS, HEAD_DIM, dtype=f32),
            vm(SHARE_HEADS, SLOTS, HEAD_DIM, dtype=f32), vm(SLOTS, 3 * SHARE), sems(12),
        ],
        11,
        "attention_back",
        after,
    )[0]


def call_input_back(layer, *args, after=()):
    return call(
        functools.partial(input_back, layer),
        args,
        [shape(*ROW), shape(1, DIM, dtype=f32)],
        [
            [vm(*QKV)] * 4, vm(*ROW), vm(*ROW, dtype=f32), GAINS, [vm(DIM, DIM)] * 3,
            vm(*ROW), vm(1, DIM, dtype=f32), vm(3, *ROW), sems(16),
        ],
        10,
        "input_back",
        after,
    )


def call_attention_weights_grad(groups, *args, after=()):
    out = (groups, 6 * DIM // groups, 128)
    return call(
        attention_weights_grad,
        args,
        [shape(*out)],
        [
            vm(SLOTS, DIM), [vm(*QKV)] * 4, [vm(PACKED, 128)] * 4, [vm(*BRANCH)] * 4, vm(*out),
            vm(SLOTS, 3 * SHARE), vm(SLOTS, SHARE), vm(DIM, SHARE, dtype=f32), sems(16),
        ],
        8,
        "attention_weights_grad",
        after,
    )[0]


def call_ffn_weights_grad(layer, groups, *args, after=()):
    out = (groups, 2, (4 * DIM + 3 * FF // 4) // groups, 128)
    return call(
        functools.partial(ffn_weights_grad, layer),
        args,
        [shape(*out)],
        [
            vm(*out), vm(PARTS + 1, DIM, FF_SHARE), vm(PARTS + 1, DIM, FF_SHARE), vm(FF_SHARE, DIM),
            vm(SLOTS, DIM), vm(SLOTS, FF), vm(SLOTS, DIM), vm(SLOTS, FF_SHARE), vm(SLOTS, FF_SHARE),
            vm(FF, SHARE, dtype=f32), sems(48),
        ],
        15,
        "ffn_weights_grad",
        after,
    )[0]


def call_join_attention(parts, gains):
    groups, rows, _ = parts[0].shape
    out = (groups, len(parts), rows + GAIN_ROWS, 128)
    return call(
        join_attention,
        (parts, gains),
        [shape(*out)],
        [vm(*gains.shape, dtype=f32), vm(*out), sems(8)],
        3,
        "join_attention",
    )[0]


def call_write_weights(groups, *args):
    rows = DIM // groups
    dims = [(1, rows, SHARE)] * 4 + [(1, rows, FF_SHARE)] * 2 + [(1, SHARE, FF // groups), (GAIN_ROWS, 128)]
    ffn, _, attn = args[:3]
    return call(
        write_weights,
        args,
        [shape(*dim, dtype=f32) for dim in dims],
        [vm(*ffn.shape), vm(*ffn.shape), vm(*attn.shape)] + [vm(*dim, dtype=f32) for dim in dims] + [sems(16)],
        3,
        "write_weights",
    )


def rotary_tables():
    lanes = np.arange(128)
    frequency = (10000.0 ** (-2.0 * (lanes % 32) / HEAD_DIM)).astype(np.float32)
    angles = np.arange(SLOTS, dtype=np.float32)[:, None] * frequency[None, :]
    sign = np.where(lanes % HEAD_DIM < 32, -1.0, 1.0).astype(np.float32)
    return np.cos(angles).astype(np.float32), (np.sin(angles) * sign).astype(np.float32)


def swap(value):
    return lax.ppermute(value, "section", [(0, 1), (1, 0)])


def to_partner(value, offset):
    return lax.ppermute(value, "seq", [(part, part ^ offset) for part in range(PARTS)])


def gathered(value):
    return [value] + [to_partner(value, offset) for offset in range(1, PARTS)]


def exchanged(blocks):
    return [blocks[0]] + [to_partner(blocks[offset], offset) for offset in range(1, PARTS)]


def later(values, *earlier):
    return lax.optimization_barrier((values, earlier))[0]


def sum_over_items(parts):
    parts = parts.reshape(-1, *parts.shape[2:])
    return lax.psum_scatter(parts, ("dp", "section"), scatter_dimension=0)


def give(value, giver):
    return lax.ppermute(value, "section", [(giver, 1 - giver)])


def on_device(
    section_input, out_cotangent, lengths, attn_gain, w_query, w_key, w_value, w_output,
    ffn_gain, w_gate, w_up, w_down,
):
    groups = lax.axis_size("dp")
    core = lax.axis_index("section")
    is_first = core == 0
    inputs = lax.dynamic_index_in_dim(section_input, core, 0, keepdims=False)
    cos, sin = (jnp.asarray(table) for table in rotary_tables())
    x_blocks = gathered(inputs)
    windows = call_pack_windows((w_query, w_key, w_value), (attn_gain, ffn_gain))
    windows = (windows, swap(windows))
    o_pair, g_pair, u_pair, d_pair = (
        (weight, swap(later(weight, *earlier)))
        for weight, *earlier in (
            (w_output, windows[1]),
            (w_gate, windows[1]),
            (w_up, windows[1], x_blocks),
            (w_down, windows[1], x_blocks),
        )
    )
    ffn = (g_pair, u_pair, d_pair)

    normed_0, heads_0, packed_0 = call_first_attention(x_blocks, lengths, cos, sin, windows)
    mixed_0 = gathered(later(packed_0, o_pair[1], g_pair[1]))
    after_0, normed_two_0, hidden_0, mid, normed_1, heads_1, packed_1, mixed_blocks = call_middle(
        x_blocks, mixed_0, lengths, cos, sin, o_pair, ffn, windows
    )
    cotangent_all = lax.all_gather(later(out_cotangent, mixed_0), "seq", axis=0)
    qkv = tuple((weight, swap(later(weight, mixed_0))) for weight in (w_query, w_key, w_value))
    mixed_rows = exchanged(mixed_blocks)
    mixed_1 = gathered(later(packed_1, mixed_rows[1]))
    output, normed_two_1, grad_after_1, gain_ffn_1, grad_blocks_1 = call_last_rows(
        mid, out_cotangent, mixed_rows, windows, o_pair, ffn, after=[pair[1] for pair in qkv]
    )
    grad_mixed_1 = exchanged(grad_blocks_1)
    normed_two_all = gathered(later(normed_two_1, grad_mixed_1[1], mixed_1))
    grad_qkv_1 = call_attention_back(grad_mixed_1, lengths, cos, sin, heads_1)
    grad_rows_1 = exchanged(grad_qkv_1)
    parts_f1 = call_ffn_weights_grad(1, groups, normed_two_all, cotangent_all, ffn, after=(grad_qkv_1[0],))
    grad_rows_1, parts_f1 = lax.optimization_barrier((grad_rows_1, parts_f1))
    sum_f1 = sum_over_items(parts_f1)
    grad_mid, gain_attn_1 = call_input_back(1, grad_rows_1, mid, grad_after_1, windows, qkv)
    grad_mid_all = gathered(grad_mid)
    grad_after_0, gain_ffn_0, grad_blocks_0 = call_first_rows_back(after_0, grad_mid, windows, o_pair, ffn)
    grad_mixed_0 = exchanged(grad_blocks_0)
    parts_f0 = call_ffn_weights_grad(
        0, groups, (normed_two_0, hidden_0), grad_mid_all, ffn, after=(grad_after_0,)
    )
    grad_mixed_0, parts_f0 = lax.optimization_barrier((grad_mixed_0, parts_f0))
    sum_f0 = sum_over_items(parts_f0)
    grad_qkv_0 = call_attention_back(grad_mixed_0, lengths, cos, sin, heads_0)
    grad_rows_0 = exchanged(grad_qkv_0)
    parts_a1 = call_attention_weights_grad(
        groups, normed_1, grad_qkv_1, mixed_1, grad_mixed_1, after=(grad_qkv_0[0],)
    )
    parts_a0 = call_attention_weights_grad(
        groups, normed_0, grad_qkv_0, mixed_0, grad_mixed_0, after=(parts_a1,)
    )
    grad_first, gain_attn_0 = call_input_back(
        0, grad_rows_0, inputs, grad_after_0, windows, qkv, after=(parts_a0,)
    )

    share = DIM // (groups * PARTS)
    gain_grads = jnp.concatenate([gain_attn_0, gain_ffn_0, gain_attn_1, gain_ffn_1], axis=0)
    gain_grads = gain_grads.reshape(2, 2, groups, PARTS, share).transpose(3, 2, 0, 1, 4)
    seq = lax.axis_index("seq")
    gain_parts = exchanged(
        [lax.dynamic_index_in_dim(gain_grads, seq ^ offset, 0, keepdims=False) for offset in range(PARTS)]
    )
    gain_rows = jnp.pad(sum(gain_parts), ((0, 0), (0, 0), (0, GAIN_ROWS - 2), (0, 128 - share)))
    sum_attn = sum_over_items(call_join_attention((parts_a0, parts_a1), gain_rows))

    def sort(of_first, of_second):
        mine = jnp.where(is_first, of_first, of_second)
        other = swap(jnp.where(is_first, of_second, of_first))
        return jnp.where(is_first, mine, other), jnp.where(is_first, other, mine)

    section_outputs = jnp.stack(sort(mid, output))[None]
    input_grads = jnp.stack(sort(grad_first, grad_mid))[None]
    g_query, g_key, g_value, g_output, g_gate, g_up, g_down, gain_sums = call_write_weights(
        groups, sum_f0, sum_f1, sum_attn, give(sum_f0, 1), give(sum_f1, 0)
    )
    gain_sums = gain_sums[:2, :share]
    return (
        section_outputs, input_grads, gain_sums[0:1], g_query, g_key, g_value, g_output, gain_sums[1:2],
        g_gate, g_up, g_down.transpose(0, 2, 1),
    )


def solution(mesh):
    return jax.shard_map(
        on_device,
        mesh=mesh,
        in_specs=(
            P("dp", "seq", None),
            P("dp", "seq", None),
            P("dp"),
            P("section", None),
            P("section", None, None),
            P("section", None, None),
            P("section", None, None),
            P("section", None, None),
            P("section", None),
            P("section", None, None),
            P("section", None, None),
            P("section", None, None),
        ),
        out_specs=(
            P("section", "dp", "seq", None),
            P("section", "dp", "seq", None),
            P("section", ("dp", "seq")),
            P("section", "dp", "seq"),
            P("section", "dp", "seq"),
            P("section", "dp", "seq"),
            P("section", "dp", "seq"),
            P("section", ("dp", "seq")),
            P("section", "dp", "seq"),
            P("section", "dp", "seq"),
            P("section", "dp", "seq"),
        ),
        check_vma=False,
    )
```

```python
import functools

import jax
import jax.numpy as jnp
import numpy as np
from jax import lax
from jax.experimental import pallas as pl
from jax.experimental.pallas import tpu as pltpu
from jax.sharding import PartitionSpec as P

DIM = 768
HEAD_DIM = 64
FF = 2048
ROWS = 160
PARTS = 4
SLOTS = ROWS * PARTS
SHARE_HEADS = 3
SHARE = SHARE_HEADS * HEAD_DIM
FF_SHARE = FF // PARTS
PACKED = SLOTS * 3 // 2
PACKED_ROWS = ROWS * 3 // 2
WINDOW = 256
QUERY_BLOCKS = ((0, 384), (384, 256))
HALVES = ((0, 320), (320, 320))

epsilon = 1e-05
masked_score = -1e30
bf16 = jnp.bfloat16
f32 = jnp.float32
MIB = 1 << 20
VMEM_MIB = 60
GAIN_ROWS = 16
COST = 10**9


def nn(left, right):
    return lax.dot_general(left, right, (((1,), (0,)), ((), ())), preferred_element_type=f32)


def nt(left, right):
    return lax.dot_general(left, right, (((1,), (1,)), ((), ())), preferred_element_type=f32)


def tn(left, right):
    return lax.dot_general(left, right, (((0,), (0,)), ((), ())), preferred_element_type=f32)


def rms_scale(values):
    return lax.rsqrt(jnp.mean(values * values, axis=-1, keepdims=True) + epsilon)


def rotate(values, cosine, signed_sine):
    width = values.shape[-1]
    lane = lax.broadcasted_iota(jnp.int32, values.shape, 1)
    ahead = pltpu.roll(values, width - 32, 1)
    behind = pltpu.roll(values, 32, 1)
    partner = jnp.where(lane % HEAD_DIM < 32, ahead, behind)
    return values * cosine + partner * signed_sine


def wide(table):
    return jnp.concatenate([table, table], axis=1)


def unpack(packed, count):
    tail = packed[count:]
    third = jnp.concatenate([tail[:, :HEAD_DIM], tail[:, HEAD_DIM:]], axis=0)
    return jnp.concatenate([packed[:count], third], axis=1)


def gain_row(gains, kind):
    rows = gains[...].astype(f32)
    return jnp.concatenate([rows[3 * kind + part : 3 * kind + part + 1, :] for part in range(3)], axis=1)


def place():
    return lax.axis_index("section"), lax.axis_index("seq")


def block_rows(index, size=ROWS):
    return pl.ds(pl.multiple_of(index * size, size), size)


def window_start(seq):
    return pl.multiple_of(((3 * seq) >> 1) * 128, 128)


class Mover:
    def __init__(self, sems, core=None):
        self.sems = sems
        self.core = core
        self.count = 0
        self.sent = []

    def next_sem(self):
        self.count += 1
        return self.sems.at[self.count - 1]

    def fetch(self, source, target):
        copy = pltpu.make_async_copy(source, target, self.next_sem())
        copy.start()
        return copy

    def fetch_all(self, sources, targets):
        return [self.fetch(source, target) for source, target in zip(sources, targets)]

    def fetch_layer(self, layer, own, other, target):
        sem = self.next_sem()

        @pl.when(self.core == layer)
        def _():
            pltpu.make_async_copy(own, target, sem).start()

        @pl.when(self.core != layer)
        def _():
            pltpu.make_async_copy(other, target, sem).start()

        return pltpu.make_async_copy(own, target, sem)

    def fetch_windows(self, layer, pair, targets):
        return [
            self.fetch_layer(layer, pair[0].at[block_rows(kind, DIM), :], pair[1].at[block_rows(kind, DIM), :], target)
            for kind, target in enumerate(targets)
        ]

    def fetch_gains(self, layer, pair, target):
        rows = slice(3 * DIM, 3 * DIM + GAIN_ROWS)
        return self.fetch_layer(layer, pair[0].at[rows, :], pair[1].at[rows, :], target)

    def fetch_ffn(self, layer, pairs, targets):
        copies = []
        for part in range(PARTS):
            span = slice(part * FF_SHARE, (part + 1) * FF_SHARE)
            (g_own, g_other), (u_own, u_other), (d_own, d_other) = pairs
            copies.append(
                (
                    self.fetch_layer(layer, g_own.at[0, :, span], g_other.at[0, :, span], targets[0].at[part]),
                    self.fetch_layer(layer, u_own.at[0, :, span], u_other.at[0, :, span], targets[1].at[part]),
                    self.fetch_layer(layer, d_own.at[0, span, :], d_other.at[0, span, :], targets[2].at[span, :]),
                )
            )
        return copies

    def send(self, source, target):
        copy = pltpu.make_async_copy(source, target, self.next_sem())
        copy.start()
        self.sent.append(copy)

    def finish(self):
        for copy in self.sent:
            copy.wait()


def wait(copies):
    for copy in copies:
        copy.wait()


def project(normed, windows, odd, cos, sin, heads, value_t):
    for first, count in QUERY_BLOCKS:
        rows = slice(first, first + count)
        block = normed[rows, :]
        cosine, sine = wide(cos[rows, :]), wide(sin[rows, :])
        for kind, window in enumerate(windows):
            result = nn(block, window[...])
            if kind < 2:
                result = rotate(result, cosine, sine)
            if kind == 0:
                result = result * HEAD_DIM ** (-0.5)
            result = jnp.where(odd, pltpu.roll(result, WINDOW - HEAD_DIM, 1), result)
            low = result.astype(bf16)
            for head in range(SHARE_HEADS):
                heads[kind, head, rows, :] = low[:, head * HEAD_DIM : (head + 1) * HEAD_DIM]
            if kind == 2:
                turned = jnp.transpose(result).astype(bf16)
                for head in range(SHARE_HEADS):
                    value_t[head, :, rows] = turned[head * HEAD_DIM : (head + 1) * HEAD_DIM, :]


def masked(scores_t, first, length):
    spots = lax.broadcasted_iota(jnp.int32, scores_t.shape, 0)
    query = first + lax.broadcasted_iota(jnp.int32, (1, scores_t.shape[1]), 1)
    bound = jnp.minimum(query + 1, length)
    return jnp.where(spots < bound, scores_t, masked_score)


def attend(heads, value_t, length, mixed_t):
    for head in range(SHARE_HEADS):
        for first, count in QUERY_BLOCKS:
            last = first + count
            scores = nt(heads[1, head, :last, :], heads[0, head, first:last, :])
            scores = masked(scores, first, length)
            exponent = jnp.exp(scores - jnp.max(scores, axis=0, keepdims=True))
            total = jnp.sum(exponent, axis=0, keepdims=True)
            mixed = nn(value_t[head, :, :last], exponent.astype(bf16))
            mixed_t[head, :, first:last] = mixed * (1.0 / total)


def untranspose(mixed_t, pair, single):
    both = jnp.concatenate([mixed_t[0], mixed_t[1]], axis=0)
    pair[...] = jnp.transpose(both).astype(bf16)
    last = jnp.concatenate([mixed_t[2], mixed_t[2]], axis=0)
    single[...] = jnp.transpose(last).astype(bf16)


def pack_all(pair, single, target):
    half = SLOTS // 2
    target[:SLOTS, :] = pair[...]
    target[SLOTS:, :] = jnp.concatenate(
        [single[:half, :HEAD_DIM], single[half:, :HEAD_DIM]], axis=1
    )


def pack_block(pair, single, index, target):
    half = ROWS // 2
    rows = block_rows(index)
    target[:ROWS, :] = pair[rows, :]
    tail = single[rows, :]
    target[ROWS:, :] = jnp.concatenate([tail[:half, :HEAD_DIM], tail[half:, :HEAD_DIM]], axis=1)


def columns_of(array, first, rows=slice(None)):
    return array[rows, first * 128 : (first + 1) * 128]


def norm_back(grad_normed, gain, normed, scale):
    scaled = grad_normed * gain
    return scale * (scaled - normed * jnp.mean(scaled * normed, axis=-1, keepdims=True))


def ffn_back_chunk(gate, up, grad_hidden):
    sigmoid = jax.nn.sigmoid(gate)
    grad_gate = grad_hidden * up * sigmoid * (1.0 + gate * (1.0 - sigmoid))
    grad_up = grad_hidden * gate * sigmoid
    return grad_gate.astype(bf16), grad_up.astype(bf16)


def pack_windows(seq_weights_h, gains_h, packed_h, packed, gains, sems):
    _, seq = place()
    move = Mover(sems)
    span = pl.ds(window_start(seq), WINDOW)
    copies = move.fetch_all(gains_h, gains)
    copies += [
        move.fetch(weight.at[0, :, span], packed.at[block_rows(kind, DIM), :])
        for kind, weight in enumerate(seq_weights_h)
    ]
    wait(copies)
    rows = [gain[:, part * WINDOW : (part + 1) * WINDOW].astype(f32) for gain in gains for part in range(3)]
    rows.append(jnp.zeros((GAIN_ROWS - 6, WINDOW), f32))
    packed[3 * DIM :, :] = jnp.concatenate(rows, axis=0).astype(bf16)
    move.send(packed, packed_h)
    move.finish()


def first_attention(
    x_h, lengths, cos_h, sin_h, windows_h,
    normed_h, heads_h, packed_h,
    x, gains, cos, sin, windows, normed, heads, packed, value_t, mixed_t, pair, single, sems,
):
    core, seq = place()
    move = Mover(sems, core)
    copy_x = move.fetch(x_h, x)
    copy_gains = move.fetch_gains(0, windows_h, gains)
    copies_qkv = move.fetch_windows(0, windows_h, windows)
    copies_table = move.fetch_all((cos_h, sin_h), (cos, sin))
    copy_gains.wait()
    gain = gain_row(gains, 0)
    copy_x.wait()
    for first, count in HALVES:
        rows = slice(first, first + count)
        block = x[rows, :].astype(f32)
        normed[rows, :] = (block * rms_scale(block) * gain).astype(bf16)
    move.send(normed, normed_h)
    wait(copies_table + copies_qkv)
    project(normed, windows, seq % 2 == 1, cos, sin, heads, value_t)
    move.send(heads, heads_h)
    attend(heads, value_t, lengths[core], mixed_t)
    untranspose(mixed_t, pair, single)
    pack_all(pair, single, packed)
    move.send(packed, packed_h)
    move.finish()


def middle(
    x_h, mixed_h, lengths, cos_h, sin_h, o_h, ffn_h, windows_h,
    after_h, normed_two_h, hidden_h, mid_h, normed_h, heads_h, packed_h, blocks_h,
    x, mixed, gains, gains_next, cos, sin, w_o, w_g, w_u, w_d, windows,
    after, normed_two, hidden, mid, normed, heads, packed, blocks, total, value_t, mixed_t, pair, single, sems,
):
    core, seq = place()
    move = Mover(sems, core)
    copy_x = move.fetch(x_h, x)
    copy_o = move.fetch_layer(0, o_h[0].at[0], o_h[1].at[0], w_o)
    copies_gain = [move.fetch_gains(0, windows_h, gains), move.fetch_gains(1, windows_h, gains_next)]
    copies_mixed = [move.fetch(mixed_h.at[part], target) for part, target in enumerate(mixed)]
    copies_ffn = move.fetch_ffn(0, ffn_h, (w_g, w_u, w_d))
    copies_qkv = move.fetch_windows(1, windows_h, windows)
    copies_table = move.fetch_all((cos_h, sin_h), (cos, sin))
    copy_x.wait()
    after[...] = x[...].astype(f32)
    copy_o.wait()
    for part, block in enumerate(mixed):
        share = w_o[part * SHARE : (part + 1) * SHARE, :]
        copies_mixed[part].wait()
        whole = unpack(block[...], SLOTS)
        for first, count in HALVES:
            rows = slice(first, first + count)
            after[rows, :] += nn(whole[rows], share)
    wait(copies_gain)
    gain_ffn = gain_row(gains, 1)
    gain_attn = gain_row(gains_next, 0)
    for first, count in HALVES:
        rows = slice(first, first + count)
        block = after[rows, :]
        normed_two[rows, :] = (block * rms_scale(block) * gain_ffn).astype(bf16)
        total[rows, :] = block
    move.send(after.at[block_rows(seq), :], after_h)
    move.send(normed_two, normed_two_h)
    for part in range(PARTS):
        wait(copies_ffn[part])
        span = slice(part * FF_SHARE, (part + 1) * FF_SHARE)
        for first, count in HALVES:
            rows = slice(first, first + count)
            block = normed_two[rows, :]
            gate = nn(block, w_g[part])
            up = nn(block, w_u[part])
            low = (gate * jax.nn.sigmoid(gate) * up).astype(bf16)
            hidden[rows, span] = low
            total[rows, :] += nn(low, w_d[span, :])
    move.send(hidden, hidden_h)
    for first, count in HALVES:
        rows = slice(first, first + count)
        low = total[rows, :].astype(bf16)
        mid[rows, :] = low
        block = low.astype(f32)
        normed[rows, :] = (block * rms_scale(block) * gain_attn).astype(bf16)
    move.send(mid.at[block_rows(seq), :], mid_h)
    move.send(normed, normed_h)
    wait(copies_table + copies_qkv)
    project(normed, windows, seq % 2 == 1, cos, sin, heads, value_t)
    move.send(heads, heads_h)
    attend(heads, value_t, lengths[core], mixed_t)
    untranspose(mixed_t, pair, single)
    for offset, (block, target) in enumerate(zip(blocks, blocks_h)):
        pack_block(pair, single, seq ^ offset, block)
        move.send(block, target)
    pack_all(pair, single, packed)
    move.send(packed, packed_h)
    move.finish()


def send_blocks(move, seq, grad_branch, w_o, blocks, blocks_h):
    for here in range(PARTS):

        @pl.when(seq == here)
        def _():
            for offset, block in enumerate(blocks):
                other = here ^ offset
                span = slice(other * SHARE, (other + 1) * SHARE)
                grad_heads = nt(grad_branch[...], w_o[span, :]).astype(bf16)
                block[...] = jnp.concatenate([grad_heads, grad_branch[:, span]], axis=1)

    for block, target in zip(blocks, blocks_h):
        move.send(block, target)


def last_rows(
    mid_h, cotangent_h, mixed_h, windows_h, o_h, ffn_h,
    output_h, normed_two_h, grad_after_h, grad_gain_h, blocks_h,
    mid, cotangent, mixed, gains, w_o, w_g, w_u, w_d,
    output, normed_two, grad_after, grad_gain, blocks, branch, hidden, sems,
):
    core, seq = place()
    move = Mover(sems, core)
    copies = move.fetch_all((mid_h, cotangent_h.at[core]), (mid, cotangent))
    copies.append(move.fetch_gains(1, windows_h, gains))
    copy_o = move.fetch_layer(1, o_h[0].at[0], o_h[1].at[0], w_o)
    copies_mixed = move.fetch_all(mixed_h, mixed)
    copies_ffn = move.fetch_ffn(1, ffn_h, (w_g, w_u, w_d))
    wait(copies)
    gain = gain_row(gains, 1)
    copy_o.wait()
    after = mid[...].astype(f32)
    for offset, block in enumerate(mixed):
        copies_mixed[offset].wait()
        after = after + nn(unpack(block[...], ROWS), w_o[block_rows(seq ^ offset, SHARE), :])
    scale = rms_scale(after)
    normed = after * scale
    low = (normed * gain).astype(bf16)
    normed_two[...] = low
    move.send(normed_two, normed_two_h)
    grad_low = cotangent[...]
    grad_normed = jnp.zeros((ROWS, DIM), f32)
    for part in range(PARTS):
        wait(copies_ffn[part])
        gate = nn(low, w_g[part])
        up = nn(low, w_u[part])
        span = slice(part * FF_SHARE, (part + 1) * FF_SHARE)
        hidden[:, span] = (gate * jax.nn.sigmoid(gate) * up).astype(bf16)
        grad_gate, grad_up = ffn_back_chunk(gate, up, nt(grad_low, w_d[span, :]))
        grad_normed = grad_normed + nt(grad_gate, w_g[part]) + nt(grad_up, w_u[part])
    grad_gain[...] = jnp.sum(grad_normed * normed, axis=0, keepdims=True)
    move.send(grad_gain, grad_gain_h)
    total = grad_low.astype(f32) + norm_back(grad_normed, gain, normed, scale)
    grad_after[...] = total
    move.send(grad_after, grad_after_h)
    branch[...] = total.astype(bf16)
    send_blocks(move, seq, branch, w_o, blocks, blocks_h)
    output[...] = (after + nn(hidden[...], w_d[...])).astype(bf16)
    move.send(output, output_h)
    move.finish()


def first_rows_back(
    after_h, grad_in_h, windows_h, o_h, ffn_h,
    grad_after_h, grad_gain_h, blocks_h,
    after_own, grad_in, gains, w_o, w_g, w_u, w_d, grad_after, grad_gain, blocks, branch, sems,
):
    core, seq = place()
    move = Mover(sems, core)
    copies = move.fetch_all((after_h, grad_in_h), (after_own, grad_in))
    copies.append(move.fetch_gains(0, windows_h, gains))
    copies_ffn = move.fetch_ffn(0, ffn_h, (w_g, w_u, w_d))
    copy_o = move.fetch_layer(0, o_h[0].at[0], o_h[1].at[0], w_o)
    wait(copies)
    gain = gain_row(gains, 1)
    after = after_own[...]
    scale = rms_scale(after)
    normed = after * scale
    low = (normed * gain).astype(bf16)
    grad_low = grad_in[...]
    grad_normed = jnp.zeros((ROWS, DIM), f32)
    for part in range(PARTS):
        wait(copies_ffn[part])
        gate = nn(low, w_g[part])
        up = nn(low, w_u[part])
        span = slice(part * FF_SHARE, (part + 1) * FF_SHARE)
        grad_gate, grad_up = ffn_back_chunk(gate, up, nt(grad_low, w_d[span, :]))
        grad_normed = grad_normed + nt(grad_gate, w_g[part]) + nt(grad_up, w_u[part])
    grad_gain[...] = jnp.sum(grad_normed * normed, axis=0, keepdims=True)
    move.send(grad_gain, grad_gain_h)
    total = grad_low.astype(f32) + norm_back(grad_normed, gain, normed, scale)
    grad_after[...] = total
    move.send(grad_after, grad_after_h)
    branch[...] = total.astype(bf16)
    copy_o.wait()
    send_blocks(move, seq, branch, w_o, blocks, blocks_h)
    move.finish()


def attention_back(
    grads_h, lengths, cos_h, sin_h, heads_h,
    blocks_h,
    grads, cos, sin, heads, grad_mixed, key_t, query_grad_t, key_grad, value_grad, whole, sems,
):
    core, seq = place()
    move = Mover(sems)
    copies_grads = move.fetch_all(grads_h, grads)
    copy_heads = move.fetch(heads_h, heads)
    copies_table = move.fetch_all((cos_h, sin_h), (cos, sin))
    key_grad[...] = jnp.zeros_like(key_grad)
    value_grad[...] = jnp.zeros_like(value_grad)
    for offset, block in enumerate(grads):
        copies_grads[offset].wait()
        low = block[:, :SHARE]
        for head in range(SHARE_HEADS):
            grad_mixed[head, block_rows(seq ^ offset), :] = low[:, head * HEAD_DIM : (head + 1) * HEAD_DIM]
    copy_heads.wait()
    length = lengths[core]

    for head in range(SHARE_HEADS):
        key_wide = heads[1, head].astype(f32)
        key_t[...] = jnp.transpose(jnp.concatenate([key_wide, key_wide], axis=1))[:HEAD_DIM].astype(bf16)
        for first, count in QUERY_BLOCKS:
            last = first + count
            query = heads[0, head, first:last, :]
            grad = grad_mixed[head, first:last, :]
            scores = nt(heads[1, head, :last, :], query)
            scores = masked(scores, first, length)
            exponent = jnp.exp(scores - jnp.max(scores, axis=0, keepdims=True))
            weights = exponent * (1.0 / jnp.sum(exponent, axis=0, keepdims=True))
            grad_weights = nt(heads[2, head, :last, :], grad)
            row_total = jnp.sum(weights * grad_weights, axis=0, keepdims=True)
            grad_scores = (weights * (grad_weights - row_total)).astype(bf16)
            value_grad[head, :last, :] += nn(weights.astype(bf16), grad)
            key_grad[head, :last, :] += nn(grad_scores, query)
            query_grad_t[head, :, first:last] = nn(key_t[:, :last], grad_scores) * HEAD_DIM ** (-0.5)

    turned = jnp.concatenate([query_grad_t[0], query_grad_t[1], query_grad_t[2], query_grad_t[2]], axis=0)
    query_side = jnp.transpose(turned)
    key_side = jnp.concatenate([key_grad[0], key_grad[1], key_grad[2], key_grad[2]], axis=1)
    value_side = jnp.concatenate([value_grad[0], value_grad[1], value_grad[2]], axis=1)
    wait(copies_table)
    cosine, sine = wide(cos[...]), wide(sin[...])
    query_side = rotate(query_side, cosine, -sine)[:, :SHARE]
    key_side = rotate(key_side, cosine, -sine)[:, :SHARE]
    whole[...] = jnp.concatenate([query_side, key_side, value_side], axis=1).astype(bf16)
    for offset, target in enumerate(blocks_h):
        move.send(whole.at[block_rows(seq ^ offset), :], target)
    move.finish()


def input_back(
    layer, blocks_h, inputs_h, grad_after_h, windows_h, qkv_h,
    grad_in_h, grad_gain_h,
    blocks, inputs, grad_after, gains, weights, grad_in, grad_gain, sides, sems,
):
    core, seq = place()
    move = Mover(sems, core)
    copies_blocks = move.fetch_all(blocks_h, blocks)
    copies = move.fetch_all((inputs_h, grad_after_h), (inputs, grad_after))
    copies.append(move.fetch_gains(layer, windows_h, gains))
    copies_qkv = [
        move.fetch_layer(layer, own.at[0], other.at[0], target) for (own, other), target in zip(qkv_h, weights)
    ]
    wait(copies_blocks)
    for here in range(PARTS):

        @pl.when(seq == here)
        def _():
            for kind in range(3):
                span = slice(kind * SHARE, (kind + 1) * SHARE)
                sides[kind] = jnp.concatenate(
                    [blocks[here ^ part][:, span] for part in range(PARTS)], axis=1
                )

    wait(copies)
    gain = gain_row(gains, 0)
    wide_inputs = inputs[...].astype(f32)
    scale = rms_scale(wide_inputs)
    normed = wide_inputs * scale
    grad_normed = jnp.zeros((ROWS, DIM), f32)
    for kind, weight in enumerate(weights):
        copies_qkv[kind].wait()
        grad_normed = grad_normed + nt(sides[kind], weight[...])
    grad_in[...] = (grad_after[...] + norm_back(grad_normed, gain, normed, scale)).astype(bf16)
    move.send(grad_in, grad_in_h)
    grad_gain[...] = jnp.sum(grad_normed * normed, axis=0, keepdims=True)
    move.send(grad_gain, grad_gain_h)
    move.finish()


def attention_weights_grad(
    own, first_h, second_h,
    result_h,
    normed, blocks, mixed, grads, packed, whole, branch, output_grad, sems,
):
    core, seq = place()
    move = Mover(sems, core)
    layer = 0 if own else 1
    normed_h, blocks_h, mixed_h, grads_h = (
        list(zip(one, two)) if isinstance(one, (list, tuple)) else (one, two) for one, two in zip(first_h, second_h)
    )

    def fetch(pairs, targets):
        return [move.fetch_layer(layer, *pair, target) for pair, target in zip(pairs, targets)]

    copies = [
        move.fetch_layer(layer, gathered_h.at[seq ^ offset], block_h, mixed[offset])
        for offset, (gathered_h, block_h) in enumerate(mixed_h)
    ]
    copies += fetch(grads_h, grads)
    copies_qkv = fetch(blocks_h, blocks) + fetch((normed_h,), (normed,))
    wait(copies)
    for offset, grad in enumerate(grads):
        branch[block_rows(seq ^ offset), :] = grad[:, SHARE:]
    for offset, block in enumerate(mixed):
        output_grad[block_rows(seq ^ offset, SHARE), :] = tn(unpack(block[...], SLOTS), branch[...])
    wait(copies_qkv)
    for offset, block in enumerate(blocks):
        whole[block_rows(seq ^ offset), :] = block[...]
    result = tn(normed[...], whole[...])
    last = jnp.concatenate([result[:, 2 * SHARE :], output_grad[...]], axis=1)
    rows = DIM // packed.shape[0]
    for group in range(packed.shape[0]):
        span = slice(group * rows, (group + 1) * rows)
        for tile in range(6):
            source = columns_of((result, last)[tile // 3], tile % 3, span)
            packed[group, tile * rows : (tile + 1) * rows, :] = source.astype(bf16)
    move.send(packed, result_h)
    move.finish()


def ffn_weights_grad(
    layer, left_h, y_h, ffn_h,
    result_h,
    packed, w_g, w_u, w_d, normed_two, normed_t, hidden, grad_out, grad_gate, grad_up, down, sems,
):
    core, seq = place()
    move = Mover(sems, core)
    (g_own, g_other), (u_own, u_other), (d_own, d_other) = ffn_h
    spans = [pl.ds(pl.multiple_of(((seq + part) & 3) * FF_SHARE, FF_SHARE), FF_SHARE) for part in range(PARTS)]
    span = spans[0]
    if layer == 0:
        copies = move.fetch_all(left_h, (normed_two, hidden))
    else:
        copies = [move.fetch(block, normed_two.at[block_rows(seq ^ offset), :]) for offset, block in enumerate(left_h)]
    copies += [move.fetch(block, grad_out.at[block_rows(seq ^ offset), :]) for offset, block in enumerate(y_h)]
    copies += [
        move.fetch_layer(layer, g_own.at[0, :, span], g_other.at[0, :, span], w_g.at[0]),
        move.fetch_layer(layer, u_own.at[0, :, span], u_other.at[0, :, span], w_u.at[0]),
        move.fetch_layer(layer, d_own.at[0, span, :], d_other.at[0, span, :], w_d),
    ]
    copies_ffn = []
    if layer == 1:
        for part in range(1, PARTS):
            copies_ffn.append(
                (
                    move.fetch_layer(
                        layer, g_own.at[0, :, spans[part]], g_other.at[0, :, spans[part]], w_g.at[part]
                    ),
                    move.fetch_layer(
                        layer, u_own.at[0, :, spans[part]], u_other.at[0, :, spans[part]], w_u.at[part]
                    ),
                )
            )
    wait(copies)
    for first, count in HALVES:
        rows = slice(first, first + count)
        block = normed_two[rows, :]
        gate, up = nn(block, w_g[0]), nn(block, w_u[0])
        grad_gate[rows, :], grad_up[rows, :] = ffn_back_chunk(gate, up, nt(grad_out[rows, :], w_d[...]))
        if layer == 1:
            hidden[rows, span] = (gate * jax.nn.sigmoid(gate) * up).astype(bf16)
    groups = packed.shape[0]
    tile_rows = DIM // groups
    normed_t[...] = jnp.transpose(normed_two[...])
    for index, grads in enumerate((grad_gate, grad_up)):
        result = nn(normed_t[...], grads[...])
        for group in range(groups):
            span = slice(group * tile_rows, (group + 1) * tile_rows)
            for tile in range(4):
                packed[group, index, tile * tile_rows : (tile + 1) * tile_rows, :] = columns_of(result, tile, span).astype(bf16)

    window = grad_out[:, pl.ds(window_start(seq), WINDOW)].astype(f32)
    columns = jnp.where(seq % 2 == 1, pltpu.roll(window, WINDOW - HEAD_DIM, 1), window)
    columns_t = jnp.transpose(columns)[:SHARE].astype(bf16)
    for part in range(PARTS):
        if layer == 1 and part > 0:
            wait(copies_ffn[part - 1])
            for first, count in HALVES:
                rows = slice(first, first + count)
                gate = nn(normed_two[rows, :], w_g[part])
                up = nn(normed_two[rows, :], w_u[part])
                hidden[rows, spans[part]] = (gate * jax.nn.sigmoid(gate) * up).astype(bf16)
        down[:, spans[part]] = nn(columns_t, hidden[:, spans[part]])
    width = FF // groups // 2
    for index in range(2):
        for group in range(groups):
            begin = (group * 2 + index) * width
            pack_down(down, begin, width, packed.at[group, index, 4 * tile_rows :, :])
    move.send(packed, result_h)
    move.finish()


def pack_down(down, begin, width, target):
    if width >= 128:
        for tile in range(width // 128):
            source = down[:, begin + tile * 128 : begin + (tile + 1) * 128]
            target[tile * SHARE : (tile + 1) * SHARE, :] = source.astype(bf16)
    else:
        rows = SHARE * width // 128
        piece = down[:, begin : begin + width]
        target[...] = jnp.concatenate(
            [piece[part * rows : (part + 1) * rows] for part in range(128 // width)], axis=1
        ).astype(bf16)


def unpack_down(source, target, begin, width):
    if width >= 128:
        for tile in range(width // 128):
            piece = source[tile * SHARE : (tile + 1) * SHARE, :]
            target[0, :, begin + tile * 128 : begin + (tile + 1) * 128] = piece.astype(f32)
    else:
        rows = SHARE * width // 128
        for part in range(128 // width):
            piece = source[:, part * width : (part + 1) * width]
            target[0, part * rows : (part + 1) * rows, begin : begin + width] = piece.astype(f32)


def add_parts(keep_h, received_h, total_h, keep, received, total, sems):
    move = Mover(sems)
    copies = [
        move.fetch_all((keep_h.at[group], received_h.at[group]), (keep.at[group], received.at[group]))
        for group in range(keep.shape[0])
    ]
    for group, pair in enumerate(copies):
        wait(pair)
        total[group] = (keep[group].astype(f32) + received[group].astype(f32)).astype(bf16)
        move.send(total.at[group], total_h.at[group])
    move.finish()


def write_weights(
    ffn_0, ffn_1, attn_h, ffn_other_0, ffn_other_1,
    q_h, k_h, v_h, o_h, g_h, u_h, d_h,
    ffn_low, ffn_high, attn, q, k, v, o, g, u, d, sems,
):
    core, _ = place()
    move = Mover(sems, core)
    copies = [
        move.fetch_layer(0, ffn_0, ffn_other_1, ffn_low),
        move.fetch_layer(0, ffn_other_0, ffn_1, ffn_high),
        move.fetch(attn_h, attn),
    ]
    wait(copies[:2])
    rows = q.shape[1]
    for index, (ffn, wide_out) in enumerate(((ffn_low, g), (ffn_high, u))):
        for tile in range(4):
            wide_out[0, :, tile * 128 : (tile + 1) * 128] = ffn[tile * rows : (tile + 1) * rows, :].astype(f32)
        width = d.shape[2] // 2
        unpack_down(ffn.at[4 * rows :, :], d, index * width, width)
    for source, target in zip((g, u, d), (g_h, u_h, d_h)):
        move.send(source, target)
    copies[2].wait()
    for index, pair in enumerate(((q, k), (v, o))):
        both = jnp.concatenate(
            [
                jnp.sum(attn[:, (index * 3 + tile) * rows : (index * 3 + tile + 1) * rows, :].astype(f32), axis=0)
                for tile in range(3)
            ],
            axis=1,
        )
        pair[0][0] = both[:, :SHARE]
        pair[1][0] = both[:, SHARE:]
    for source, target in zip((q, k, v, o), (q_h, k_h, v_h, o_h)):
        move.send(source, target)
    move.finish()


def shape(*dims, dtype=bf16):
    return jax.ShapeDtypeStruct(dims, dtype)


def vm(*dims, dtype=bf16):
    return pltpu.VMEM(dims, dtype)


def call(body, args, outs, scratch, micros, name, after=(), vmem=VMEM_MIB):
    leaves, tree = jax.tree.flatten(args)
    out_leaves, out_tree = jax.tree.flatten(outs)
    scratch_leaves, scratch_tree = jax.tree.flatten(scratch)
    count_in, count_all = len(leaves), len(leaves) + len(after)

    def kernel(*refs):
        ins = jax.tree.unflatten(tree, refs[:count_in])
        results = jax.tree.unflatten(out_tree, refs[count_all : count_all + len(out_leaves)])
        temps = jax.tree.unflatten(scratch_tree, refs[count_all + len(out_leaves) :])
        body(*ins, *results, *temps)

    def spec(leaf):
        small = leaf.dtype == jnp.int32
        return pl.BlockSpec(memory_space=pltpu.SMEM if small else pltpu.HBM)

    results = pl.pallas_call(
        kernel,
        out_shape=out_leaves,
        in_specs=[spec(leaf) for leaf in leaves] + [pl.BlockSpec(memory_space=pltpu.HBM)] * len(after),
        out_specs=[pl.BlockSpec(memory_space=pltpu.HBM)] * len(out_leaves),
        scratch_shapes=scratch_leaves,
        compiler_params=pltpu.CompilerParams(vmem_limit_bytes=vmem * MIB),
        cost_estimate=pl.CostEstimate(flops=micros * COST, bytes_accessed=10**4, transcendentals=0),
        name=name,
    )(*leaves, *after)
    return jax.tree.unflatten(out_tree, results)


def sems(count):
    return pltpu.SemaphoreType.DMA((count,))


GAINS = vm(GAIN_ROWS, WINDOW)
TABLES = [vm(SLOTS, 128, dtype=f32)] * 2
HEADS = (3, SHARE_HEADS, SLOTS, HEAD_DIM)
WEIGHTS = [vm(DIM, DIM), vm(PARTS, DIM, FF_SHARE), vm(PARTS, DIM, FF_SHARE), vm(FF, DIM)]
ATTEND = [
    vm(SHARE_HEADS, HEAD_DIM, SLOTS),
    vm(SHARE_HEADS, HEAD_DIM, SLOTS, dtype=f32),
    vm(SLOTS, 128),
    vm(SLOTS, 128),
]
WINDOWS = [vm(DIM, WINDOW)] * 3
ROW = (ROWS, DIM)
BRANCH = (ROWS, 2 * SHARE)
QKV = (ROWS, 3 * SHARE)


def call_pack_windows(weights, gains):
    rows = 3 * DIM + GAIN_ROWS
    return call(
        pack_windows,
        (weights, gains),
        [shape(rows, WINDOW)],
        [vm(rows, WINDOW), [vm(1, DIM)] * 2, sems(8)],
        3,
        "pack_windows",
    )[0]


def call_first_attention(*args, after=()):
    return call(
        first_attention,
        args,
        [shape(SLOTS, DIM), shape(*HEADS), shape(PACKED, 128)],
        [vm(SLOTS, DIM), GAINS, *TABLES, WINDOWS, vm(SLOTS, DIM), vm(*HEADS), vm(PACKED, 128), *ATTEND, sems(16)],
        10,
        "first_attention",
        after,
    )


def call_middle(*args):
    return call(
        middle,
        args,
        [
            shape(*ROW, dtype=f32), shape(SLOTS, DIM), shape(SLOTS, FF), shape(*ROW), shape(SLOTS, DIM),
            shape(*HEADS), shape(PACKED, 128), [shape(PACKED_ROWS, 128)] * 4,
        ],
        [
            vm(SLOTS, DIM), [vm(PACKED, 128)] * 4, GAINS, GAINS, *TABLES, *WEIGHTS, WINDOWS,
            vm(SLOTS, DIM, dtype=f32), vm(SLOTS, DIM), vm(SLOTS, FF), vm(SLOTS, DIM), vm(SLOTS, DIM),
            vm(*HEADS), vm(PACKED, 128), [vm(PACKED_ROWS, 128)] * 4, vm(SLOTS, DIM, dtype=f32), *ATTEND, sems(48),
        ],
        20,
        "middle",
    )


def call_last_rows(*args, after=()):
    return call(
        last_rows,
        args,
        [shape(*ROW), shape(*ROW), shape(*ROW, dtype=f32), shape(1, DIM, dtype=f32), [shape(*BRANCH)] * 4],
        [
            vm(*ROW), vm(*ROW), [vm(PACKED_ROWS, 128)] * 4, GAINS, *WEIGHTS,
            vm(*ROW), vm(*ROW), vm(*ROW, dtype=f32), vm(1, DIM, dtype=f32), [vm(*BRANCH)] * 4,
            vm(*ROW), vm(ROWS, FF), sems(32),
        ],
        11,
        "last_rows",
        after,
    )


def call_first_rows_back(*args, after=()):
    return call(
        first_rows_back,
        args,
        [shape(*ROW, dtype=f32), shape(1, DIM, dtype=f32), [shape(*BRANCH)] * 4],
        [
            vm(*ROW, dtype=f32), vm(*ROW), GAINS, *WEIGHTS,
            vm(*ROW, dtype=f32), vm(1, DIM, dtype=f32), [vm(*BRANCH)] * 4, vm(*ROW), sems(32),
        ],
        10,
        "first_rows_back",
        after,
    )


def call_attention_back(*args, after=()):
    return call(
        attention_back,
        args,
        [[shape(*QKV)] * 4],
        [
            [vm(*BRANCH)] * 4, *TABLES, vm(*HEADS), vm(SHARE_HEADS, SLOTS, HEAD_DIM), vm(HEAD_DIM, SLOTS),
            vm(SHARE_HEADS, HEAD_DIM, SLOTS, dtype=f32), vm(SHARE_HEADS, SLOTS, HEAD_DIM, dtype=f32),
            vm(SHARE_HEADS, SLOTS, HEAD_DIM, dtype=f32), vm(SLOTS, 3 * SHARE), sems(12),
        ],
        11,
        "attention_back",
        after,
    )[0]


def call_input_back(layer, *args, after=()):
    return call(
        functools.partial(input_back, layer),
        args,
        [shape(*ROW), shape(1, DIM, dtype=f32)],
        [
            [vm(*QKV)] * 4, vm(*ROW), vm(*ROW, dtype=f32), GAINS, [vm(DIM, DIM)] * 3,
            vm(*ROW), vm(1, DIM, dtype=f32), vm(3, *ROW), sems(16),
        ],
        10,
        "input_back",
        after,
    )


def call_attention_weights_grad(own, groups, *args, after=()):
    out = (groups, 6 * DIM // groups, 128)
    return call(
        functools.partial(attention_weights_grad, own),
        args,
        [shape(*out)],
        [
            vm(SLOTS, DIM), [vm(*QKV)] * 4, [vm(PACKED, 128)] * 4, [vm(*BRANCH)] * 4, vm(*out),
            vm(SLOTS, 3 * SHARE), vm(SLOTS, SHARE), vm(DIM, SHARE, dtype=f32), sems(16),
        ],
        8,
        "attention_weights_grad",
        after,
    )[0]


def call_ffn_weights_grad(layer, groups, *args, after=()):
    out = (groups, 2, (4 * DIM + 3 * FF // 4) // groups, 128)
    return call(
        functools.partial(ffn_weights_grad, layer),
        args,
        [shape(*out)],
        [
            vm(*out), vm(PARTS, DIM, FF_SHARE), vm(PARTS, DIM, FF_SHARE), vm(FF_SHARE, DIM),
            vm(SLOTS, DIM), vm(DIM, SLOTS), vm(SLOTS, FF), vm(SLOTS, DIM), vm(SLOTS, FF_SHARE), vm(SLOTS, FF_SHARE),
            vm(SHARE, FF, dtype=f32), sems(48),
        ],
        15,
        "ffn_weights_grad",
        after,
    )[0]


def call_add_parts(keep, received, after):
    dims = keep.shape
    return call(
        add_parts,
        (keep, received),
        [shape(*dims)],
        [vm(*dims), vm(*dims), vm(*dims), sems(3 * dims[0])],
        3,
        "add_parts",
        after,
    )[0]


def call_write_weights(groups, *args):
    rows = DIM // groups
    dims = [(1, rows, SHARE)] * 4 + [(1, rows, FF_SHARE)] * 2 + [(1, SHARE, FF // groups)]
    ffn, _, attn = args[:3]
    return call(
        write_weights,
        args,
        [shape(*dim, dtype=f32) for dim in dims],
        [vm(*ffn.shape), vm(*ffn.shape), vm(*attn.shape)] + [vm(*dim, dtype=f32) for dim in dims] + [sems(16)],
        3,
        "write_weights",
        vmem=24,
    )


def rotary_tables():
    lanes = np.arange(128)
    frequency = (10000.0 ** (-2.0 * (lanes % 32) / HEAD_DIM)).astype(np.float32)
    angles = np.arange(SLOTS, dtype=np.float32)[:, None] * frequency[None, :]
    sign = np.where(lanes % HEAD_DIM < 32, -1.0, 1.0).astype(np.float32)
    return np.cos(angles).astype(np.float32), (np.sin(angles) * sign).astype(np.float32)


def swap(value):
    return lax.ppermute(value, "section", [(0, 1), (1, 0)])


def to_partner(value, offset):
    return lax.ppermute(value, "seq", [(part, part ^ offset) for part in range(PARTS)])


def gathered(value):
    return [value] + [to_partner(value, offset) for offset in range(1, PARTS)]


def exchanged(blocks):
    return [blocks[0]] + [to_partner(blocks[offset], offset) for offset in range(1, PARTS)]


def later(values, *earlier):
    return lax.optimization_barrier((values, earlier))[0]


def sum_over_items(parts):
    parts = parts.reshape(-1, *parts.shape[2:])
    return lax.psum_scatter(parts, ("dp", "section"), scatter_dimension=0)


def give(value, giver):
    return lax.ppermute(value, "section", [(giver, 1 - giver)])


def on_device(
    section_input, out_cotangent, lengths, attn_gain, w_query, w_key, w_value, w_output,
    ffn_gain, w_gate, w_up, w_down,
):
    groups = lax.axis_size("dp")
    core = lax.axis_index("section")
    is_first = core == 0
    inputs = lax.dynamic_index_in_dim(section_input, core, 0, keepdims=False)
    cotangent = lax.dynamic_index_in_dim(out_cotangent, core, 0, keepdims=False)
    cos, sin = (jnp.asarray(table) for table in rotary_tables())
    windows = call_pack_windows((w_query, w_key, w_value), (attn_gain, ffn_gain))
    windows = (windows, swap(windows))
    x_all = lax.all_gather(later(inputs, windows[0]), "seq", axis=0, tiled=True)
    o_pair, *ffn = ((weight, swap(later(weight, x_all, windows[1]))) for weight in (w_output, w_gate, w_up, w_down))

    normed_0, heads_0, packed_0 = call_first_attention(x_all, lengths, cos, sin, windows)
    mixed_0 = lax.all_gather(packed_0, "seq", axis=0)
    after_0, normed_two_0, hidden_0, mid, normed_1, heads_1, packed_1, mixed_blocks = call_middle(
        x_all, mixed_0, lengths, cos, sin, o_pair, ffn, windows
    )
    others = [pair[1] for pair in (o_pair, *ffn)]
    cotangent_all = gathered(later(cotangent, mixed_0, others))
    q_pair, k_pair = ((weight, swap(later(weight, mixed_0, others))) for weight in (w_query, w_key))
    qkv = (q_pair, k_pair, (w_value, swap(later(w_value, cotangent_all, q_pair[1]))))
    mixed_rows = exchanged(later(mixed_blocks, cotangent_all[1:], q_pair[1], k_pair[1]))
    mixed_1 = gathered(later(packed_1, mixed_rows[1]))
    output, normed_two_1, grad_after_1, gain_ffn_1, grad_blocks_1 = call_last_rows(
        mid, out_cotangent, mixed_rows, windows, o_pair, ffn
    )
    grad_mixed_1 = exchanged(later(grad_blocks_1, mixed_1))
    normed_two_all = gathered(later(normed_two_1, grad_mixed_1[1], mixed_1))
    grad_qkv_1 = call_attention_back(grad_mixed_1, lengths, cos, sin, heads_1)
    grad_rows_1 = exchanged(grad_qkv_1)
    parts_f1 = call_ffn_weights_grad(1, groups, normed_two_all, cotangent_all, ffn, after=(grad_qkv_1[0],))
    grad_rows_1, parts_f1 = lax.optimization_barrier((grad_rows_1, parts_f1))
    sum_f1 = sum_over_items(parts_f1)
    grad_mid, gain_attn_1 = call_input_back(1, grad_rows_1, mid, grad_after_1, windows, qkv)
    grad_mid_all = gathered(grad_mid)
    grad_after_0, gain_ffn_0, grad_blocks_0 = call_first_rows_back(after_0, grad_mid, windows, o_pair, ffn)
    grad_mixed_0 = exchanged(grad_blocks_0)
    parts_f0 = call_ffn_weights_grad(
        0, groups, (normed_two_0, hidden_0), grad_mid_all, ffn, after=(grad_after_0,)
    )
    grad_mixed_0, parts_f0 = lax.optimization_barrier((grad_mixed_0, parts_f0))
    sum_f0 = sum_over_items(later(parts_f0, sum_f1))
    grad_qkv_0 = call_attention_back(grad_mixed_0, lengths, cos, sin, heads_0)
    grad_rows_0 = exchanged(grad_qkv_0)
    of_layers = (
        (normed_0, grad_qkv_0, [mixed_0] * PARTS, grad_mixed_0),
        (normed_1, grad_qkv_1, mixed_1, grad_mixed_1),
    )
    send_a = call_attention_weights_grad(False, groups, *of_layers, after=(grad_qkv_0[0],))
    keep_a = call_attention_weights_grad(True, groups, *of_layers, after=(send_a,))
    send_a, keep_a = lax.optimization_barrier((send_a, keep_a))
    received_a = swap(send_a)
    grad_first, gain_attn_0 = call_input_back(0, grad_rows_0, inputs, grad_after_0, windows, qkv, after=(keep_a,))
    added_a = call_add_parts(keep_a, received_a, after=(grad_first,))
    sums_a = lax.all_to_all(added_a, "dp", split_axis=0, concat_axis=0, tiled=True)

    share = DIM // (groups * PARTS)
    gain_grads = jnp.concatenate([gain_attn_0, gain_ffn_0, gain_attn_1, gain_ffn_1], axis=0)
    gain_grads = later(gain_grads, added_a).reshape(2, 2, groups, PARTS, share)
    seq, here = lax.axis_index("seq"), lax.axis_index("dp")
    gain_grads = sum(
        exchanged([lax.dynamic_index_in_dim(gain_grads, seq ^ offset, 3, keepdims=False) for offset in range(PARTS)])
    )
    gain_grads = jnp.where(is_first, gain_grads[0], gain_grads[1]) + swap(
        jnp.where(is_first, gain_grads[1], gain_grads[0])
    )
    gain_sums = lax.dynamic_index_in_dim(gain_grads, here, 1, keepdims=False)
    for offset in range(1, groups):
        part = lax.dynamic_index_in_dim(gain_grads, lax.rem(here + offset, groups), 1, keepdims=False)
        gain_sums = gain_sums + lax.ppermute(
            part, "dp", [(group, (group + offset) % groups) for group in range(groups)]
        )

    def sort(of_first, of_second):
        mine = jnp.where(is_first, of_first, of_second)
        other = swap(jnp.where(is_first, of_second, of_first))
        return jnp.where(is_first, mine, other), jnp.where(is_first, other, mine)

    section_outputs = jnp.stack(sort(*later((mid, output), grad_qkv_0[0])))[None]
    input_grads = jnp.stack(sort(grad_first, grad_mid))[None]
    g_query, g_key, g_value, g_output, g_gate, g_up, g_down = call_write_weights(
        groups, sum_f0, sum_f1, sums_a, give(sum_f0, 1), give(sum_f1, 0)
    )
    return (
        section_outputs, input_grads, gain_sums[0:1], g_query, g_key, g_value, g_output, gain_sums[1:2],
        g_gate, g_up, g_down.transpose(0, 2, 1),
    )


def solution(mesh):
    return jax.shard_map(
        on_device,
        mesh=mesh,
        in_specs=(
            P("dp", "seq", None),
            P("dp", "seq", None),
            P("dp"),
            P("section", None),
            P("section", None, None),
            P("section", None, None),
            P("section", None, None),
            P("section", None, None),
            P("section", None),
            P("section", None, None),
            P("section", None, None),
            P("section", None, None),
        ),
        out_specs=(
            P("section", "dp", "seq", None),
            P("section", "dp", "seq", None),
            P("section", ("dp", "seq")),
            P("section", "dp", "seq"),
            P("section", "dp", "seq"),
            P("section", "dp", "seq"),
            P("section", "dp", "seq"),
            P("section", ("dp", "seq")),
            P("section", "dp", "seq"),
            P("section", "dp", "seq"),
            P("section", "dp", "seq"),
        ),
        check_vma=False,
    )
```

```python
import functools

import jax
import jax.numpy as jnp
import numpy as np
from jax import lax
from jax.experimental import pallas as pl
from jax.experimental.pallas import tpu as pltpu
from jax.sharding import PartitionSpec as P

DIM = 768
HEAD_DIM = 64
FF = 2048
ROWS = 160
PARTS = 4
SLOTS = ROWS * PARTS
SHARE_HEADS = 3
SHARE = SHARE_HEADS * HEAD_DIM
FF_SHARE = FF // PARTS
PACKED = SLOTS * 3 // 2
PACKED_ROWS = ROWS * 3 // 2
WINDOW = 256
QUERY_BLOCKS = ((0, 384), (384, 256))
HALVES = ((0, 320), (320, 320))

epsilon = 1e-05
masked_score = -1e30
bf16 = jnp.bfloat16
f32 = jnp.float32
MIB = 1 << 20
VMEM_MIB = 60
GAIN_ROWS = 16
COST = 10**9


def nn(left, right):
    return lax.dot_general(left, right, (((1,), (0,)), ((), ())), preferred_element_type=f32)


def nt(left, right):
    return lax.dot_general(left, right, (((1,), (1,)), ((), ())), preferred_element_type=f32)


def tn(left, right):
    return lax.dot_general(left, right, (((0,), (0,)), ((), ())), preferred_element_type=f32)


def rms_scale(values):
    return lax.rsqrt(jnp.mean(values * values, axis=-1, keepdims=True) + epsilon)


def rotate(values, cosine, signed_sine):
    width = values.shape[-1]
    lane = lax.broadcasted_iota(jnp.int32, values.shape, 1)
    ahead = pltpu.roll(values, width - 32, 1)
    behind = pltpu.roll(values, 32, 1)
    partner = jnp.where(lane % HEAD_DIM < 32, ahead, behind)
    return values * cosine + partner * signed_sine


def wide(table):
    return jnp.concatenate([table, table], axis=1)


def unpack(packed, count):
    tail = packed[count:]
    third = jnp.concatenate([tail[:, :HEAD_DIM], tail[:, HEAD_DIM:]], axis=0)
    return jnp.concatenate([packed[:count], third], axis=1)


def gain_row(gains, kind):
    rows = gains[...].astype(f32)
    return jnp.concatenate([rows[3 * kind + part : 3 * kind + part + 1, :] for part in range(3)], axis=1)


def place():
    return lax.axis_index("section"), lax.axis_index("seq")


def block_rows(index, size=ROWS):
    return pl.ds(pl.multiple_of(index * size, size), size)


def window_start(seq):
    return pl.multiple_of(((3 * seq) >> 1) * 128, 128)


class Mover:
    def __init__(self, sems, core=None):
        self.sems = sems
        self.core = core
        self.count = 0
        self.sent = []

    def next_sem(self):
        self.count += 1
        return self.sems.at[self.count - 1]

    def fetch(self, source, target):
        copy = pltpu.make_async_copy(source, target, self.next_sem())
        copy.start()
        return copy

    def fetch_all(self, sources, targets):
        return [self.fetch(source, target) for source, target in zip(sources, targets)]

    def fetch_layer(self, layer, own, other, target):
        sem = self.next_sem()

        @pl.when(self.core == layer)
        def _():
            pltpu.make_async_copy(own, target, sem).start()

        @pl.when(self.core != layer)
        def _():
            pltpu.make_async_copy(other, target, sem).start()

        return pltpu.make_async_copy(own, target, sem)

    def fetch_windows(self, layer, pair, targets):
        return [
            self.fetch_layer(layer, pair[0].at[block_rows(kind, DIM), :], pair[1].at[block_rows(kind, DIM), :], target)
            for kind, target in enumerate(targets)
        ]

    def fetch_gains(self, layer, pair, target):
        rows = slice(3 * DIM, 3 * DIM + GAIN_ROWS)
        return self.fetch_layer(layer, pair[0].at[rows, :], pair[1].at[rows, :], target)

    def fetch_ffn(self, layer, pairs, targets):
        copies = []
        for part in range(PARTS):
            span = slice(part * FF_SHARE, (part + 1) * FF_SHARE)
            (g_own, g_other), (u_own, u_other), (d_own, d_other) = pairs
            copies.append(
                (
                    self.fetch_layer(layer, g_own.at[0, :, span], g_other.at[0, :, span], targets[0].at[part]),
                    self.fetch_layer(layer, u_own.at[0, :, span], u_other.at[0, :, span], targets[1].at[part]),
                    self.fetch_layer(layer, d_own.at[0, span, :], d_other.at[0, span, :], targets[2].at[span, :]),
                )
            )
        return copies

    def send(self, source, target):
        copy = pltpu.make_async_copy(source, target, self.next_sem())
        copy.start()
        self.sent.append(copy)

    def finish(self):
        for copy in self.sent:
            copy.wait()


def wait(copies):
    for copy in copies:
        copy.wait()


def project(normed, windows, odd, cos, sin, heads, value_t):
    for first, count in QUERY_BLOCKS:
        rows = slice(first, first + count)
        block = normed[rows, :]
        cosine, sine = wide(cos[rows, :]), wide(sin[rows, :])
        for kind, window in enumerate(windows):
            result = nn(block, window[...])
            if kind < 2:
                result = rotate(result, cosine, sine)
            if kind == 0:
                result = result * HEAD_DIM ** (-0.5)
            result = jnp.where(odd, pltpu.roll(result, WINDOW - HEAD_DIM, 1), result)
            low = result.astype(bf16)
            for head in range(SHARE_HEADS):
                heads[kind, head, rows, :] = low[:, head * HEAD_DIM : (head + 1) * HEAD_DIM]
            if kind == 2:
                turned = jnp.transpose(result).astype(bf16)
                for head in range(SHARE_HEADS):
                    value_t[head, :, rows] = turned[head * HEAD_DIM : (head + 1) * HEAD_DIM, :]


def masked(scores_t, first, length):
    spots = lax.broadcasted_iota(jnp.int32, scores_t.shape, 0)
    query = first + lax.broadcasted_iota(jnp.int32, (1, scores_t.shape[1]), 1)
    bound = jnp.minimum(query + 1, length)
    return jnp.where(spots < bound, scores_t, masked_score)


def attend(heads, value_t, length, mixed_t):
    for head in range(SHARE_HEADS):
        for first, count in QUERY_BLOCKS:
            last = first + count
            scores = nt(heads[1, head, :last, :], heads[0, head, first:last, :])
            scores = masked(scores, first, length)
            exponent = jnp.exp(scores - jnp.max(scores, axis=0, keepdims=True))
            total = jnp.sum(exponent, axis=0, keepdims=True)
            mixed = nn(value_t[head, :, :last], exponent.astype(bf16))
            mixed_t[head, :, first:last] = mixed * (1.0 / total)


def untranspose(mixed_t, pair, single):
    both = jnp.concatenate([mixed_t[0], mixed_t[1]], axis=0)
    pair[...] = jnp.transpose(both).astype(bf16)
    last = jnp.concatenate([mixed_t[2], mixed_t[2]], axis=0)
    single[...] = jnp.transpose(last).astype(bf16)


def pack_all(pair, single, target):
    half = SLOTS // 2
    target[:SLOTS, :] = pair[...]
    target[SLOTS:, :] = jnp.concatenate(
        [single[:half, :HEAD_DIM], single[half:, :HEAD_DIM]], axis=1
    )


def pack_block(pair, single, index, target):
    half = ROWS // 2
    rows = block_rows(index)
    target[:ROWS, :] = pair[rows, :]
    tail = single[rows, :]
    target[ROWS:, :] = jnp.concatenate([tail[:half, :HEAD_DIM], tail[half:, :HEAD_DIM]], axis=1)


def columns_of(array, first, rows=slice(None)):
    return array[rows, first * 128 : (first + 1) * 128]


def norm_back(grad_normed, gain, normed, scale):
    scaled = grad_normed * gain
    return scale * (scaled - normed * jnp.mean(scaled * normed, axis=-1, keepdims=True))


def ffn_back_chunk(gate, up, grad_hidden):
    sigmoid = jax.nn.sigmoid(gate)
    grad_gate = grad_hidden * up * sigmoid * (1.0 + gate * (1.0 - sigmoid))
    grad_up = grad_hidden * gate * sigmoid
    return grad_gate.astype(bf16), grad_up.astype(bf16)


def pack_windows(seq_weights_h, gains_h, packed_h, packed, gains, sems):
    _, seq = place()
    move = Mover(sems)
    span = pl.ds(window_start(seq), WINDOW)
    copies = move.fetch_all(gains_h, gains)
    copies += [
        move.fetch(weight.at[0, :, span], packed.at[block_rows(kind, DIM), :])
        for kind, weight in enumerate(seq_weights_h)
    ]
    wait(copies)
    rows = [gain[:, part * WINDOW : (part + 1) * WINDOW].astype(f32) for gain in gains for part in range(3)]
    rows.append(jnp.zeros((GAIN_ROWS - 6, WINDOW), f32))
    packed[3 * DIM :, :] = jnp.concatenate(rows, axis=0).astype(bf16)
    move.send(packed, packed_h)
    move.finish()


def first_attention(
    x_h, lengths, cos_h, sin_h, windows_h,
    normed_h, heads_h, packed_h,
    x, gains, cos, sin, windows, normed, heads, packed, value_t, mixed_t, pair, single, sems,
):
    core, seq = place()
    move = Mover(sems, core)
    copy_x = move.fetch(x_h, x)
    copy_gains = move.fetch_gains(0, windows_h, gains)
    copies_qkv = move.fetch_windows(0, windows_h, windows)
    copies_table = move.fetch_all((cos_h, sin_h), (cos, sin))
    copy_gains.wait()
    gain = gain_row(gains, 0)
    copy_x.wait()
    for first, count in HALVES:
        rows = slice(first, first + count)
        block = x[rows, :].astype(f32)
        normed[rows, :] = (block * rms_scale(block) * gain).astype(bf16)
    move.send(normed, normed_h)
    wait(copies_table + copies_qkv)
    project(normed, windows, seq % 2 == 1, cos, sin, heads, value_t)
    move.send(heads, heads_h)
    attend(heads, value_t, lengths[core], mixed_t)
    untranspose(mixed_t, pair, single)
    pack_all(pair, single, packed)
    move.send(packed, packed_h)
    move.finish()


def middle(
    x_h, mixed_h, lengths, cos_h, sin_h, o_h, ffn_h, windows_h,
    after_h, normed_two_h, hidden_h, mid_h, normed_h, heads_h, packed_h, blocks_h,
    x, mixed, gains, gains_next, cos, sin, w_o, w_g, w_u, w_d, windows,
    after, normed_two, hidden, mid, normed, heads, packed, blocks, total, value_t, mixed_t, pair, single, sems,
):
    core, seq = place()
    move = Mover(sems, core)
    copy_x = move.fetch(x_h, x)
    copy_o = move.fetch_layer(0, o_h[0].at[0], o_h[1].at[0], w_o)
    copies_gain = [move.fetch_gains(0, windows_h, gains), move.fetch_gains(1, windows_h, gains_next)]
    copies_mixed = [move.fetch(mixed_h.at[part], target) for part, target in enumerate(mixed)]
    copies_ffn = move.fetch_ffn(0, ffn_h, (w_g, w_u, w_d))
    copies_qkv = move.fetch_windows(1, windows_h, windows)
    copies_table = move.fetch_all((cos_h, sin_h), (cos, sin))
    copy_x.wait()
    after[...] = x[...].astype(f32)
    copy_o.wait()
    for part, block in enumerate(mixed):
        share = w_o[part * SHARE : (part + 1) * SHARE, :]
        copies_mixed[part].wait()
        whole = unpack(block[...], SLOTS)
        for first, count in HALVES:
            rows = slice(first, first + count)
            after[rows, :] += nn(whole[rows], share)
    wait(copies_gain)
    gain_ffn = gain_row(gains, 1)
    gain_attn = gain_row(gains_next, 0)
    for first, count in HALVES:
        rows = slice(first, first + count)
        block = after[rows, :]
        normed_two[rows, :] = (block * rms_scale(block) * gain_ffn).astype(bf16)
        total[rows, :] = block
    move.send(after.at[block_rows(seq), :], after_h)
    move.send(normed_two, normed_two_h)
    for part in range(PARTS):
        wait(copies_ffn[part])
        span = slice(part * FF_SHARE, (part + 1) * FF_SHARE)
        for first, count in HALVES:
            rows = slice(first, first + count)
            block = normed_two[rows, :]
            gate = nn(block, w_g[part])
            up = nn(block, w_u[part])
            low = (gate * jax.nn.sigmoid(gate) * up).astype(bf16)
            hidden[rows, span] = low
            total[rows, :] += nn(low, w_d[span, :])
    move.send(hidden, hidden_h)
    for first, count in HALVES:
        rows = slice(first, first + count)
        low = total[rows, :].astype(bf16)
        mid[rows, :] = low
        block = low.astype(f32)
        normed[rows, :] = (block * rms_scale(block) * gain_attn).astype(bf16)
    move.send(mid.at[block_rows(seq), :], mid_h)
    move.send(normed, normed_h)
    wait(copies_table + copies_qkv)
    project(normed, windows, seq % 2 == 1, cos, sin, heads, value_t)
    move.send(heads, heads_h)
    attend(heads, value_t, lengths[core], mixed_t)
    untranspose(mixed_t, pair, single)
    for offset, (block, target) in enumerate(zip(blocks, blocks_h)):
        pack_block(pair, single, seq ^ offset, block)
        move.send(block, target)
    pack_all(pair, single, packed)
    move.send(packed, packed_h)
    move.finish()


def send_blocks(move, seq, grad_branch, w_o, blocks, blocks_h):
    for here in range(PARTS):

        @pl.when(seq == here)
        def _():
            for offset, block in enumerate(blocks):
                other = here ^ offset
                span = slice(other * SHARE, (other + 1) * SHARE)
                grad_heads = nt(grad_branch[...], w_o[span, :]).astype(bf16)
                block[...] = jnp.concatenate([grad_heads, grad_branch[:, span]], axis=1)

    for block, target in zip(blocks, blocks_h):
        move.send(block, target)


def last_rows(
    mid_h, cotangent_h, mixed_h, windows_h, o_h, ffn_h,
    after_h, hidden_h, normed_two_h, grad_after_h, grad_gain_h, blocks_h,
    mid, cotangent, mixed, gains, w_o, w_g, w_u, w_d,
    after_out, normed_two, grad_after, grad_gain, blocks, branch, hidden, sems,
):
    core, seq = place()
    move = Mover(sems, core)
    copies = move.fetch_all((mid_h, cotangent_h.at[core]), (mid, cotangent))
    copies.append(move.fetch_gains(1, windows_h, gains))
    copy_o = move.fetch_layer(1, o_h[0].at[0], o_h[1].at[0], w_o)
    copies_mixed = move.fetch_all(mixed_h, mixed)
    copies_ffn = move.fetch_ffn(1, ffn_h, (w_g, w_u, w_d))
    wait(copies)
    gain = gain_row(gains, 1)
    copy_o.wait()
    after = mid[...].astype(f32)
    for offset, block in enumerate(mixed):
        copies_mixed[offset].wait()
        after = after + nn(unpack(block[...], ROWS), w_o[block_rows(seq ^ offset, SHARE), :])
    scale = rms_scale(after)
    normed = after * scale
    low = (normed * gain).astype(bf16)
    after_out[...] = after
    move.send(after_out, after_h)
    normed_two[...] = low
    move.send(normed_two, normed_two_h)
    grad_low = cotangent[...]
    grad_normed = jnp.zeros((ROWS, DIM), f32)
    for part in range(PARTS):
        wait(copies_ffn[part])
        gate = nn(low, w_g[part])
        up = nn(low, w_u[part])
        span = slice(part * FF_SHARE, (part + 1) * FF_SHARE)
        hidden[:, span] = (gate * jax.nn.sigmoid(gate) * up).astype(bf16)
        grad_gate, grad_up = ffn_back_chunk(gate, up, nt(grad_low, w_d[span, :]))
        grad_normed = grad_normed + nt(grad_gate, w_g[part]) + nt(grad_up, w_u[part])
    move.send(hidden, hidden_h)
    grad_gain[...] = jnp.sum(grad_normed * normed, axis=0, keepdims=True)
    move.send(grad_gain, grad_gain_h)
    total = grad_low.astype(f32) + norm_back(grad_normed, gain, normed, scale)
    grad_after[...] = total
    move.send(grad_after, grad_after_h)
    branch[...] = total.astype(bf16)
    send_blocks(move, seq, branch, w_o, blocks, blocks_h)
    move.finish()


def last_output(after_h, hidden_h, d_h, output_h, after, hidden, w_d, output, sems):
    core, _ = place()
    move = Mover(sems, core)
    wait(move.fetch_all((after_h, hidden_h), (after, hidden)) + [move.fetch_layer(1, d_h[0].at[0], d_h[1].at[0], w_d)])
    output[...] = (after[...] + nn(hidden[...], w_d[...])).astype(bf16)
    move.send(output, output_h)
    move.finish()


def first_rows_back(
    after_h, grad_in_h, windows_h, o_h, ffn_h,
    grad_after_h, grad_gain_h, blocks_h,
    after_own, grad_in, gains, w_o, w_g, w_u, w_d, grad_after, grad_gain, blocks, branch, sems,
):
    core, seq = place()
    move = Mover(sems, core)
    copies = move.fetch_all((after_h, grad_in_h), (after_own, grad_in))
    copies.append(move.fetch_gains(0, windows_h, gains))
    copies_ffn = move.fetch_ffn(0, ffn_h, (w_g, w_u, w_d))
    copy_o = move.fetch_layer(0, o_h[0].at[0], o_h[1].at[0], w_o)
    wait(copies)
    gain = gain_row(gains, 1)
    after = after_own[...]
    scale = rms_scale(after)
    normed = after * scale
    low = (normed * gain).astype(bf16)
    grad_low = grad_in[...]
    grad_normed = jnp.zeros((ROWS, DIM), f32)
    for part in range(PARTS):
        wait(copies_ffn[part])
        gate = nn(low, w_g[part])
        up = nn(low, w_u[part])
        span = slice(part * FF_SHARE, (part + 1) * FF_SHARE)
        grad_gate, grad_up = ffn_back_chunk(gate, up, nt(grad_low, w_d[span, :]))
        grad_normed = grad_normed + nt(grad_gate, w_g[part]) + nt(grad_up, w_u[part])
    grad_gain[...] = jnp.sum(grad_normed * normed, axis=0, keepdims=True)
    move.send(grad_gain, grad_gain_h)
    total = grad_low.astype(f32) + norm_back(grad_normed, gain, normed, scale)
    grad_after[...] = total
    move.send(grad_after, grad_after_h)
    branch[...] = total.astype(bf16)
    copy_o.wait()
    send_blocks(move, seq, branch, w_o, blocks, blocks_h)
    move.finish()


def attention_back(
    grads_h, lengths, cos_h, sin_h, heads_h,
    blocks_h,
    grads, cos, sin, heads, grad_mixed, key_t, query_grad_t, key_grad, value_grad, whole, sems,
):
    core, seq = place()
    move = Mover(sems)
    copies_grads = move.fetch_all(grads_h, grads)
    copy_heads = move.fetch(heads_h, heads)
    copies_table = move.fetch_all((cos_h, sin_h), (cos, sin))
    key_grad[...] = jnp.zeros_like(key_grad)
    value_grad[...] = jnp.zeros_like(value_grad)
    for offset, block in enumerate(grads):
        copies_grads[offset].wait()
        low = block[:, :SHARE]
        for head in range(SHARE_HEADS):
            grad_mixed[head, block_rows(seq ^ offset), :] = low[:, head * HEAD_DIM : (head + 1) * HEAD_DIM]
    copy_heads.wait()
    length = lengths[core]

    for head in range(SHARE_HEADS):
        key_wide = heads[1, head].astype(f32)
        key_t[...] = jnp.transpose(jnp.concatenate([key_wide, key_wide], axis=1))[:HEAD_DIM].astype(bf16)
        for first, count in QUERY_BLOCKS:
            last = first + count
            query = heads[0, head, first:last, :]
            grad = grad_mixed[head, first:last, :]
            scores = nt(heads[1, head, :last, :], query)
            scores = masked(scores, first, length)
            exponent = jnp.exp(scores - jnp.max(scores, axis=0, keepdims=True))
            weights = exponent * (1.0 / jnp.sum(exponent, axis=0, keepdims=True))
            grad_weights = nt(heads[2, head, :last, :], grad)
            row_total = jnp.sum(weights * grad_weights, axis=0, keepdims=True)
            grad_scores = (weights * (grad_weights - row_total)).astype(bf16)
            value_grad[head, :last, :] += nn(weights.astype(bf16), grad)
            key_grad[head, :last, :] += nn(grad_scores, query)
            query_grad_t[head, :, first:last] = nn(key_t[:, :last], grad_scores) * HEAD_DIM ** (-0.5)

    turned = jnp.concatenate([query_grad_t[0], query_grad_t[1], query_grad_t[2], query_grad_t[2]], axis=0)
    query_side = jnp.transpose(turned)
    key_side = jnp.concatenate([key_grad[0], key_grad[1], key_grad[2], key_grad[2]], axis=1)
    value_side = jnp.concatenate([value_grad[0], value_grad[1], value_grad[2]], axis=1)
    wait(copies_table)
    cosine, sine = wide(cos[...]), wide(sin[...])
    query_side = rotate(query_side, cosine, -sine)[:, :SHARE]
    key_side = rotate(key_side, cosine, -sine)[:, :SHARE]
    whole[...] = jnp.concatenate([query_side, key_side, value_side], axis=1).astype(bf16)
    for offset, target in enumerate(blocks_h):
        move.send(whole.at[block_rows(seq ^ offset), :], target)
    move.finish()


def input_back(
    layer, blocks_h, inputs_h, grad_after_h, windows_h, qkv_h,
    grad_in_h, grad_gain_h,
    blocks, inputs, grad_after, gains, weights, grad_in, grad_gain, sides, sems,
):
    core, seq = place()
    move = Mover(sems, core)
    copies_blocks = move.fetch_all(blocks_h, blocks)
    copies = move.fetch_all((inputs_h, grad_after_h), (inputs, grad_after))
    copies.append(move.fetch_gains(layer, windows_h, gains))
    copies_qkv = [
        move.fetch_layer(layer, own.at[0], other.at[0], target) for (own, other), target in zip(qkv_h, weights)
    ]
    wait(copies_blocks)
    for here in range(PARTS):

        @pl.when(seq == here)
        def _():
            for kind in range(3):
                span = slice(kind * SHARE, (kind + 1) * SHARE)
                sides[kind] = jnp.concatenate(
                    [blocks[here ^ part][:, span] for part in range(PARTS)], axis=1
                )

    wait(copies)
    gain = gain_row(gains, 0)
    wide_inputs = inputs[...].astype(f32)
    scale = rms_scale(wide_inputs)
    normed = wide_inputs * scale
    grad_normed = jnp.zeros((ROWS, DIM), f32)
    for kind, weight in enumerate(weights):
        copies_qkv[kind].wait()
        grad_normed = grad_normed + nt(sides[kind], weight[...])
    grad_in[...] = (grad_after[...] + norm_back(grad_normed, gain, normed, scale)).astype(bf16)
    move.send(grad_in, grad_in_h)
    grad_gain[...] = jnp.sum(grad_normed * normed, axis=0, keepdims=True)
    move.send(grad_gain, grad_gain_h)
    move.finish()


def attention_weights_grad(
    own, first_h, second_h,
    result_h,
    normed, blocks, mixed, grads, packed, whole, branch, output_grad, sems,
):
    core, seq = place()
    move = Mover(sems, core)
    layer = 0 if own else 1
    normed_h, blocks_h, mixed_h, grads_h = (
        list(zip(one, two)) if isinstance(one, (list, tuple)) else (one, two) for one, two in zip(first_h, second_h)
    )

    def fetch(pairs, targets):
        return [move.fetch_layer(layer, *pair, target) for pair, target in zip(pairs, targets)]

    copies = [
        move.fetch_layer(layer, gathered_h.at[seq ^ offset], block_h, mixed[offset])
        for offset, (gathered_h, block_h) in enumerate(mixed_h)
    ]
    copies += fetch(grads_h, grads)
    copies_qkv = fetch(blocks_h, blocks) + fetch((normed_h,), (normed,))
    wait(copies)
    for offset, grad in enumerate(grads):
        branch[block_rows(seq ^ offset), :] = grad[:, SHARE:]
    for offset, block in enumerate(mixed):
        output_grad[block_rows(seq ^ offset, SHARE), :] = tn(unpack(block[...], SLOTS), branch[...])
    wait(copies_qkv)
    for offset, block in enumerate(blocks):
        whole[block_rows(seq ^ offset), :] = block[...]
    result = tn(normed[...], whole[...])
    last = jnp.concatenate([result[:, 2 * SHARE :], output_grad[...]], axis=1)
    rows = DIM // packed.shape[0]
    for group in range(packed.shape[0]):
        span = slice(group * rows, (group + 1) * rows)
        for tile in range(6):
            source = columns_of((result, last)[tile // 3], tile % 3, span)
            packed[group, tile * rows : (tile + 1) * rows, :] = source.astype(bf16)
    move.send(packed, result_h)
    move.finish()


def ffn_weights_grad(
    layer, left_h, y_h, ffn_h,
    result_h,
    packed, w_g, w_u, w_d, normed_two, normed_t, hidden, grad_out, grad_gate, grad_up, down, sems,
):
    core, seq = place()
    move = Mover(sems, core)
    (g_own, g_other), (u_own, u_other), (d_own, d_other) = ffn_h
    spans = [pl.ds(pl.multiple_of(((seq + part) & 3) * FF_SHARE, FF_SHARE), FF_SHARE) for part in range(PARTS)]
    span = spans[0]
    if layer == 0:
        copies = move.fetch_all(left_h, (normed_two, hidden))
    else:
        copies = [move.fetch(block, normed_two.at[block_rows(seq ^ offset), :]) for offset, block in enumerate(left_h)]
    copies += [move.fetch(block, grad_out.at[block_rows(seq ^ offset), :]) for offset, block in enumerate(y_h)]
    copies += [
        move.fetch_layer(layer, g_own.at[0, :, span], g_other.at[0, :, span], w_g.at[0]),
        move.fetch_layer(layer, u_own.at[0, :, span], u_other.at[0, :, span], w_u.at[0]),
        move.fetch_layer(layer, d_own.at[0, span, :], d_other.at[0, span, :], w_d),
    ]
    copies_ffn = []
    if layer == 1:
        for part in range(1, PARTS):
            copies_ffn.append(
                (
                    move.fetch_layer(
                        layer, g_own.at[0, :, spans[part]], g_other.at[0, :, spans[part]], w_g.at[part]
                    ),
                    move.fetch_layer(
                        layer, u_own.at[0, :, spans[part]], u_other.at[0, :, spans[part]], w_u.at[part]
                    ),
                )
            )
    wait(copies)
    for first, count in HALVES:
        rows = slice(first, first + count)
        block = normed_two[rows, :]
        gate, up = nn(block, w_g[0]), nn(block, w_u[0])
        grad_gate[rows, :], grad_up[rows, :] = ffn_back_chunk(gate, up, nt(grad_out[rows, :], w_d[...]))
        if layer == 1:
            hidden[rows, span] = (gate * jax.nn.sigmoid(gate) * up).astype(bf16)
    groups = packed.shape[0]
    tile_rows = DIM // groups
    normed_t[...] = jnp.transpose(normed_two[...])
    for index, grads in enumerate((grad_gate, grad_up)):
        result = nn(normed_t[...], grads[...])
        for group in range(groups):
            span = slice(group * tile_rows, (group + 1) * tile_rows)
            for tile in range(4):
                packed[group, index, tile * tile_rows : (tile + 1) * tile_rows, :] = columns_of(result, tile, span).astype(bf16)

    window = grad_out[:, pl.ds(window_start(seq), WINDOW)].astype(f32)
    columns = jnp.where(seq % 2 == 1, pltpu.roll(window, WINDOW - HEAD_DIM, 1), window)
    columns_t = jnp.transpose(columns)[:SHARE].astype(bf16)
    for part in range(PARTS):
        if layer == 1 and part > 0:
            wait(copies_ffn[part - 1])
            for first, count in HALVES:
                rows = slice(first, first + count)
                gate = nn(normed_two[rows, :], w_g[part])
                up = nn(normed_two[rows, :], w_u[part])
                hidden[rows, spans[part]] = (gate * jax.nn.sigmoid(gate) * up).astype(bf16)
        down[:, spans[part]] = nn(columns_t, hidden[:, spans[part]])
    width = FF // groups // 2
    for index in range(2):
        for group in range(groups):
            begin = (group * 2 + index) * width
            pack_down(down, begin, width, packed.at[group, index, 4 * tile_rows :, :])
    move.send(packed, result_h)
    move.finish()


def pack_down(down, begin, width, target):
    if width >= 128:
        for tile in range(width // 128):
            source = down[:, begin + tile * 128 : begin + (tile + 1) * 128]
            target[tile * SHARE : (tile + 1) * SHARE, :] = source.astype(bf16)
    else:
        rows = SHARE * width // 128
        piece = down[:, begin : begin + width]
        target[...] = jnp.concatenate(
            [piece[part * rows : (part + 1) * rows] for part in range(128 // width)], axis=1
        ).astype(bf16)


def unpack_down(source, target, begin, width):
    if width >= 128:
        for tile in range(width // 128):
            piece = source[tile * SHARE : (tile + 1) * SHARE, :]
            target[0, :, begin + tile * 128 : begin + (tile + 1) * 128] = piece.astype(f32)
    else:
        rows = SHARE * width // 128
        for part in range(128 // width):
            piece = source[:, part * width : (part + 1) * width]
            target[0, part * rows : (part + 1) * rows, begin : begin + width] = piece.astype(f32)


def add_parts(keep_h, received_h, total_h, keep, received, total, sems):
    move = Mover(sems)
    copies = [
        move.fetch_all((keep_h.at[group], received_h.at[group]), (keep.at[group], received.at[group]))
        for group in range(keep.shape[0])
    ]
    for group, pair in enumerate(copies):
        wait(pair)
        total[group] = (keep[group].astype(f32) + received[group].astype(f32)).astype(bf16)
        move.send(total.at[group], total_h.at[group])
    move.finish()


def write_weights(
    ffn_0, ffn_1, attn_h, ffn_other_0, ffn_other_1,
    q_h, k_h, v_h, o_h, g_h, u_h, d_h,
    ffn_low, ffn_high, attn, q, k, v, o, g, u, d, sems,
):
    core, _ = place()
    move = Mover(sems, core)
    copies = [
        move.fetch_layer(0, ffn_0, ffn_other_1, ffn_low),
        move.fetch_layer(0, ffn_other_0, ffn_1, ffn_high),
        move.fetch(attn_h, attn),
    ]
    wait(copies[:2])
    rows = q.shape[1]
    for index, (ffn, wide_out) in enumerate(((ffn_low, g), (ffn_high, u))):
        for tile in range(4):
            wide_out[0, :, tile * 128 : (tile + 1) * 128] = ffn[tile * rows : (tile + 1) * rows, :].astype(f32)
        width = d.shape[2] // 2
        unpack_down(ffn.at[4 * rows :, :], d, index * width, width)
    for source, target in zip((g, u, d), (g_h, u_h, d_h)):
        move.send(source, target)
    copies[2].wait()
    for index, pair in enumerate(((q, k), (v, o))):
        both = jnp.concatenate(
            [
                jnp.sum(attn[:, (index * 3 + tile) * rows : (index * 3 + tile + 1) * rows, :].astype(f32), axis=0)
                for tile in range(3)
            ],
            axis=1,
        )
        pair[0][0] = both[:, :SHARE]
        pair[1][0] = both[:, SHARE:]
    for source, target in zip((q, k, v, o), (q_h, k_h, v_h, o_h)):
        move.send(source, target)
    move.finish()


def shape(*dims, dtype=bf16):
    return jax.ShapeDtypeStruct(dims, dtype)


def vm(*dims, dtype=bf16):
    return pltpu.VMEM(dims, dtype)


def call(body, args, outs, scratch, micros, name, after=(), vmem=VMEM_MIB):
    leaves, tree = jax.tree.flatten(args)
    out_leaves, out_tree = jax.tree.flatten(outs)
    scratch_leaves, scratch_tree = jax.tree.flatten(scratch)
    count_in, count_all = len(leaves), len(leaves) + len(after)

    def kernel(*refs):
        ins = jax.tree.unflatten(tree, refs[:count_in])
        results = jax.tree.unflatten(out_tree, refs[count_all : count_all + len(out_leaves)])
        temps = jax.tree.unflatten(scratch_tree, refs[count_all + len(out_leaves) :])
        body(*ins, *results, *temps)

    def spec(leaf):
        small = leaf.dtype == jnp.int32
        return pl.BlockSpec(memory_space=pltpu.SMEM if small else pltpu.HBM)

    results = pl.pallas_call(
        kernel,
        out_shape=out_leaves,
        in_specs=[spec(leaf) for leaf in leaves] + [pl.BlockSpec(memory_space=pltpu.HBM)] * len(after),
        out_specs=[pl.BlockSpec(memory_space=pltpu.HBM)] * len(out_leaves),
        scratch_shapes=scratch_leaves,
        compiler_params=pltpu.CompilerParams(vmem_limit_bytes=vmem * MIB),
        cost_estimate=pl.CostEstimate(flops=micros * COST, bytes_accessed=10**4, transcendentals=0),
        name=name,
    )(*leaves, *after)
    return jax.tree.unflatten(out_tree, results)


def sems(count):
    return pltpu.SemaphoreType.DMA((count,))


GAINS = vm(GAIN_ROWS, WINDOW)
TABLES = [vm(SLOTS, 128, dtype=f32)] * 2
HEADS = (3, SHARE_HEADS, SLOTS, HEAD_DIM)
WEIGHTS = [vm(DIM, DIM), vm(PARTS, DIM, FF_SHARE), vm(PARTS, DIM, FF_SHARE), vm(FF, DIM)]
ATTEND = [
    vm(SHARE_HEADS, HEAD_DIM, SLOTS),
    vm(SHARE_HEADS, HEAD_DIM, SLOTS, dtype=f32),
    vm(SLOTS, 128),
    vm(SLOTS, 128),
]
WINDOWS = [vm(DIM, WINDOW)] * 3
ROW = (ROWS, DIM)
BRANCH = (ROWS, 2 * SHARE)
QKV = (ROWS, 3 * SHARE)


def call_pack_windows(weights, gains):
    rows = 3 * DIM + GAIN_ROWS
    return call(
        pack_windows,
        (weights, gains),
        [shape(rows, WINDOW)],
        [vm(rows, WINDOW), [vm(1, DIM)] * 2, sems(8)],
        3,
        "pack_windows",
    )[0]


def call_first_attention(*args, after=()):
    return call(
        first_attention,
        args,
        [shape(SLOTS, DIM), shape(*HEADS), shape(PACKED, 128)],
        [vm(SLOTS, DIM), GAINS, *TABLES, WINDOWS, vm(SLOTS, DIM), vm(*HEADS), vm(PACKED, 128), *ATTEND, sems(16)],
        10,
        "first_attention",
        after,
    )


def call_middle(*args):
    return call(
        middle,
        args,
        [
            shape(*ROW, dtype=f32), shape(SLOTS, DIM), shape(SLOTS, FF), shape(*ROW), shape(SLOTS, DIM),
            shape(*HEADS), shape(PACKED, 128), [shape(PACKED_ROWS, 128)] * 4,
        ],
        [
            vm(SLOTS, DIM), [vm(PACKED, 128)] * 4, GAINS, GAINS, *TABLES, *WEIGHTS, WINDOWS,
            vm(SLOTS, DIM, dtype=f32), vm(SLOTS, DIM), vm(SLOTS, FF), vm(SLOTS, DIM), vm(SLOTS, DIM),
            vm(*HEADS), vm(PACKED, 128), [vm(PACKED_ROWS, 128)] * 4, vm(SLOTS, DIM, dtype=f32), *ATTEND, sems(48),
        ],
        20,
        "middle",
    )


def call_last_rows(*args, after=()):
    return call(
        last_rows,
        args,
        [
            shape(*ROW, dtype=f32), shape(ROWS, FF), shape(*ROW), shape(*ROW, dtype=f32),
            shape(1, DIM, dtype=f32), [shape(*BRANCH)] * 4,
        ],
        [
            vm(*ROW), vm(*ROW), [vm(PACKED_ROWS, 128)] * 4, GAINS, *WEIGHTS,
            vm(*ROW, dtype=f32), vm(*ROW), vm(*ROW, dtype=f32), vm(1, DIM, dtype=f32), [vm(*BRANCH)] * 4,
            vm(*ROW), vm(ROWS, FF), sems(32),
        ],
        11,
        "last_rows",
        after,
    )


def call_last_output(*args, after=()):
    return call(
        last_output,
        args,
        [shape(*ROW)],
        [vm(*ROW, dtype=f32), vm(ROWS, FF), vm(FF, DIM), vm(*ROW), sems(4)],
        4,
        "last_output",
        after,
    )[0]


def call_first_rows_back(*args, after=()):
    return call(
        first_rows_back,
        args,
        [shape(*ROW, dtype=f32), shape(1, DIM, dtype=f32), [shape(*BRANCH)] * 4],
        [
            vm(*ROW, dtype=f32), vm(*ROW), GAINS, *WEIGHTS,
            vm(*ROW, dtype=f32), vm(1, DIM, dtype=f32), [vm(*BRANCH)] * 4, vm(*ROW), sems(32),
        ],
        10,
        "first_rows_back",
        after,
    )


def call_attention_back(*args, after=()):
    return call(
        attention_back,
        args,
        [[shape(*QKV)] * 4],
        [
            [vm(*BRANCH)] * 4, *TABLES, vm(*HEADS), vm(SHARE_HEADS, SLOTS, HEAD_DIM), vm(HEAD_DIM, SLOTS),
            vm(SHARE_HEADS, HEAD_DIM, SLOTS, dtype=f32), vm(SHARE_HEADS, SLOTS, HEAD_DIM, dtype=f32),
            vm(SHARE_HEADS, SLOTS, HEAD_DIM, dtype=f32), vm(SLOTS, 3 * SHARE), sems(12),
        ],
        11,
        "attention_back",
        after,
    )[0]


def call_input_back(layer, *args, after=()):
    return call(
        functools.partial(input_back, layer),
        args,
        [shape(*ROW), shape(1, DIM, dtype=f32)],
        [
            [vm(*QKV)] * 4, vm(*ROW), vm(*ROW, dtype=f32), GAINS, [vm(DIM, DIM)] * 3,
            vm(*ROW), vm(1, DIM, dtype=f32), vm(3, *ROW), sems(16),
        ],
        10,
        "input_back",
        after,
    )


def call_attention_weights_grad(own, groups, *args, after=()):
    out = (groups, 6 * DIM // groups, 128)
    return call(
        functools.partial(attention_weights_grad, own),
        args,
        [shape(*out)],
        [
            vm(SLOTS, DIM), [vm(*QKV)] * 4, [vm(PACKED, 128)] * 4, [vm(*BRANCH)] * 4, vm(*out),
            vm(SLOTS, 3 * SHARE), vm(SLOTS, SHARE), vm(DIM, SHARE, dtype=f32), sems(16),
        ],
        8,
        "attention_weights_grad",
        after,
    )[0]


def call_ffn_weights_grad(layer, groups, *args, after=()):
    out = (groups, 2, (4 * DIM + 3 * FF // 4) // groups, 128)
    return call(
        functools.partial(ffn_weights_grad, layer),
        args,
        [shape(*out)],
        [
            vm(*out), vm(PARTS, DIM, FF_SHARE), vm(PARTS, DIM, FF_SHARE), vm(FF_SHARE, DIM),
            vm(SLOTS, DIM), vm(DIM, SLOTS), vm(SLOTS, FF), vm(SLOTS, DIM), vm(SLOTS, FF_SHARE), vm(SLOTS, FF_SHARE),
            vm(SHARE, FF, dtype=f32), sems(48),
        ],
        15,
        "ffn_weights_grad",
        after,
    )[0]


def call_add_parts(keep, received, after):
    dims = keep.shape
    return call(
        add_parts,
        (keep, received),
        [shape(*dims)],
        [vm(*dims), vm(*dims), vm(*dims), sems(3 * dims[0])],
        3,
        "add_parts",
        after,
    )[0]


def call_write_weights(groups, *args):
    rows = DIM // groups
    dims = [(1, rows, SHARE)] * 4 + [(1, rows, FF_SHARE)] * 2 + [(1, SHARE, FF // groups)]
    ffn, _, attn = args[:3]
    return call(
        write_weights,
        args,
        [shape(*dim, dtype=f32) for dim in dims],
        [vm(*ffn.shape), vm(*ffn.shape), vm(*attn.shape)] + [vm(*dim, dtype=f32) for dim in dims] + [sems(16)],
        3,
        "write_weights",
        vmem=24,
    )


def rotary_tables():
    lanes = np.arange(128)
    frequency = (10000.0 ** (-2.0 * (lanes % 32) / HEAD_DIM)).astype(np.float32)
    angles = np.arange(SLOTS, dtype=np.float32)[:, None] * frequency[None, :]
    sign = np.where(lanes % HEAD_DIM < 32, -1.0, 1.0).astype(np.float32)
    return np.cos(angles).astype(np.float32), (np.sin(angles) * sign).astype(np.float32)


def swap(value):
    return lax.ppermute(value, "section", [(0, 1), (1, 0)])


def to_partner(value, offset):
    return lax.ppermute(value, "seq", [(part, part ^ offset) for part in range(PARTS)])


def gathered(value):
    return [value] + [to_partner(value, offset) for offset in range(1, PARTS)]


def exchanged(blocks):
    return [blocks[0]] + [to_partner(blocks[offset], offset) for offset in range(1, PARTS)]


def later(values, *earlier):
    return lax.optimization_barrier((values, earlier))[0]


def sum_over_items(parts):
    parts = parts.reshape(-1, *parts.shape[2:])
    return lax.psum_scatter(parts, ("dp", "section"), scatter_dimension=0)


def give(value, giver):
    return lax.ppermute(value, "section", [(giver, 1 - giver)])


def on_device(
    section_input, out_cotangent, lengths, attn_gain, w_query, w_key, w_value, w_output,
    ffn_gain, w_gate, w_up, w_down,
):
    groups = lax.axis_size("dp")
    core = lax.axis_index("section")
    is_first = core == 0
    inputs = lax.dynamic_index_in_dim(section_input, core, 0, keepdims=False)
    cotangent = lax.dynamic_index_in_dim(out_cotangent, core, 0, keepdims=False)
    cos, sin = (jnp.asarray(table) for table in rotary_tables())
    windows = call_pack_windows((w_query, w_key, w_value), (attn_gain, ffn_gain))
    windows = (windows, swap(windows))
    x_all = lax.all_gather(later(inputs, windows[0]), "seq", axis=0, tiled=True)
    o_pair, *ffn = ((weight, swap(later(weight, x_all, windows[1]))) for weight in (w_output, w_gate, w_up, w_down))

    normed_0, heads_0, packed_0 = call_first_attention(x_all, lengths, cos, sin, windows)
    mixed_0 = lax.all_gather(packed_0, "seq", axis=0)
    after_0, normed_two_0, hidden_0, mid, normed_1, heads_1, packed_1, mixed_blocks = call_middle(
        x_all, mixed_0, lengths, cos, sin, o_pair, ffn, windows
    )
    others = [pair[1] for pair in (o_pair, *ffn)]
    cotangent_all = gathered(later(cotangent, mixed_0, others))
    q_pair, k_pair = ((weight, swap(later(weight, mixed_0, others))) for weight in (w_query, w_key))
    qkv = (q_pair, k_pair, (w_value, swap(later(w_value, cotangent_all, q_pair[1]))))
    mixed_rows = exchanged(later(mixed_blocks, cotangent_all[1:], q_pair[1], k_pair[1]))
    mixed_1 = gathered(later(packed_1, mixed_rows[1]))
    after_1, hidden_1, normed_two_1, grad_after_1, gain_ffn_1, grad_blocks_1 = call_last_rows(
        mid, out_cotangent, mixed_rows, windows, o_pair, ffn
    )
    grad_mixed_1 = exchanged(later(grad_blocks_1, mixed_1))
    normed_two_all = gathered(later(normed_two_1, grad_mixed_1[1], mixed_1))
    grad_qkv_1 = call_attention_back(grad_mixed_1, lengths, cos, sin, heads_1)
    grad_rows_1 = exchanged(grad_qkv_1)
    parts_f1 = call_ffn_weights_grad(1, groups, normed_two_all, cotangent_all, ffn, after=(grad_qkv_1[0],))
    grad_rows_1, parts_f1 = lax.optimization_barrier((grad_rows_1, parts_f1))
    sum_f1 = sum_over_items(parts_f1)
    grad_mid, gain_attn_1 = call_input_back(1, grad_rows_1, mid, grad_after_1, windows, qkv)
    grad_mid_all = gathered(grad_mid)
    grad_after_0, gain_ffn_0, grad_blocks_0 = call_first_rows_back(after_0, grad_mid, windows, o_pair, ffn)
    grad_mixed_0 = exchanged(grad_blocks_0)
    parts_f0 = call_ffn_weights_grad(
        0, groups, (normed_two_0, hidden_0), grad_mid_all, ffn, after=(grad_after_0,)
    )
    grad_mixed_0, parts_f0 = lax.optimization_barrier((grad_mixed_0, parts_f0))
    sum_f0 = sum_over_items(later(parts_f0, sum_f1))
    grad_qkv_0 = call_attention_back(grad_mixed_0, lengths, cos, sin, heads_0)
    grad_rows_0 = exchanged(grad_qkv_0)
    of_layers = (
        (normed_0, grad_qkv_0, [mixed_0] * PARTS, grad_mixed_0),
        (normed_1, grad_qkv_1, mixed_1, grad_mixed_1),
    )
    send_a = call_attention_weights_grad(False, groups, *of_layers, after=(grad_qkv_0[0],))
    keep_a = call_attention_weights_grad(True, groups, *of_layers, after=(send_a,))
    send_a, keep_a = lax.optimization_barrier((send_a, keep_a))
    received_a = swap(send_a)
    grad_first, gain_attn_0 = call_input_back(0, grad_rows_0, inputs, grad_after_0, windows, qkv, after=(keep_a,))
    added_a = call_add_parts(keep_a, received_a, after=(grad_first,))
    sums_a = lax.all_to_all(added_a, "dp", split_axis=0, concat_axis=0, tiled=True)

    share = DIM // (groups * PARTS)
    gain_grads = jnp.concatenate([gain_attn_0, gain_ffn_0, gain_attn_1, gain_ffn_1], axis=0)
    gain_grads = later(gain_grads, added_a).reshape(2, 2, groups, PARTS, share)
    seq, here = lax.axis_index("seq"), lax.axis_index("dp")
    gain_grads = sum(
        exchanged([lax.dynamic_index_in_dim(gain_grads, seq ^ offset, 3, keepdims=False) for offset in range(PARTS)])
    )
    gain_grads = jnp.where(is_first, gain_grads[0], gain_grads[1]) + swap(
        jnp.where(is_first, gain_grads[1], gain_grads[0])
    )
    gain_sums = lax.dynamic_index_in_dim(gain_grads, here, 1, keepdims=False)
    for offset in range(1, groups):
        part = lax.dynamic_index_in_dim(gain_grads, lax.rem(here + offset, groups), 1, keepdims=False)
        gain_sums = gain_sums + lax.ppermute(
            part, "dp", [(group, (group + offset) % groups) for group in range(groups)]
        )

    def sort(of_first, of_second):
        mine = jnp.where(is_first, of_first, of_second)
        other = swap(jnp.where(is_first, of_second, of_first))
        return jnp.where(is_first, mine, other), jnp.where(is_first, other, mine)

    output = call_last_output(after_1, hidden_1, ffn[2], after=(added_a,))
    section_outputs = jnp.stack(sort(mid, output))[None]
    input_grads = jnp.stack(sort(grad_first, grad_mid))[None]
    g_query, g_key, g_value, g_output, g_gate, g_up, g_down = call_write_weights(
        groups, sum_f0, sum_f1, sums_a, give(sum_f0, 1), give(sum_f1, 0)
    )
    return (
        section_outputs, input_grads, gain_sums[0:1], g_query, g_key, g_value, g_output, gain_sums[1:2],
        g_gate, g_up, g_down.transpose(0, 2, 1),
    )


def solution(mesh):
    return jax.shard_map(
        on_device,
        mesh=mesh,
        in_specs=(
            P("dp", "seq", None),
            P("dp", "seq", None),
            P("dp"),
            P("section", None),
            P("section", None, None),
            P("section", None, None),
            P("section", None, None),
            P("section", None, None),
            P("section", None),
            P("section", None, None),
            P("section", None, None),
            P("section", None, None),
        ),
        out_specs=(
            P("section", "dp", "seq", None),
            P("section", "dp", "seq", None),
            P("section", ("dp", "seq")),
            P("section", "dp", "seq"),
            P("section", "dp", "seq"),
            P("section", "dp", "seq"),
            P("section", "dp", "seq"),
            P("section", ("dp", "seq")),
            P("section", "dp", "seq"),
            P("section", "dp", "seq"),
            P("section", "dp", "seq"),
        ),
        check_vma=False,
    )
```
